32 devices in a mesh: grp: 2 (over core), seq: 4 (over z), head: 4 (over y, x).
Axes of the slice: x: 2, y: 2, z: 4, core: 2. Of those that a mesh axis runs over, the one named last changes fastest.
Arguments:
- queries: bfloat16 [768, 64, 128], P('seq', ('grp', 'head')), may hold values from -6 to 6
- keys: bfloat16 [768, 64, 128], P('seq', ('grp', 'head')), may hold values from -6 to 6
- values: bfloat16 [768, 64, 128], P('seq', ('grp', 'head')), may hold values from -6 to 6
- documents: int32 [768], P('seq'), may hold values from 0 to 3, never falling along the last dimension, each value on 1 to 576 neighbouring positions
- feature_map: float32 [64, 128, 128], P(('grp', 'head')), may hold values from -8 to 8
Outputs:
- teacher_out: bfloat16 [768, 64, 128], P('seq', ('grp', 'head'))
- student_out: bfloat16 [768, 64, 128], P('seq', ('grp', 'head'))
- loss: float32 [], replicated
- feature_grad: float32 [64, 128, 128], P(('grp', 'head'))
The draws below stay inside these ranges and needn't reach their ends.
All inputs are finite; a program needn't handle non-finite values.
Results may differ from the reference program's by a relative error of at most 0.006.
Values may be sent and summed in bfloat16 or wider, within the bound.
No kernel may reach another device: no remote copies, remote signals or barrier semaphores. Data moves between devices by JAX's collectives and lax.ppermute only.
A program may use at most 192 MiB of HBM per device.

```python
import math
import jax
import jax.numpy as jnp
import numpy as np
from jax import lax

HEADS = 64
HEAD_DIM = 128
FEAT = 128
WINDOW = 64
DOCS = 4
TOKENS = 768
DOC_MOST = 576


def paired_draw(key):
    base_key = jax.random.fold_in(key, 17)
    first_key, second_key = jax.random.split(base_key)
    shape = (TOKENS, HEADS, HEAD_DIM)
    query_base = jnp.clip(jax.random.normal(first_key, shape, jnp.float32), -4.0, 4.0)
    key_base = jnp.clip(jax.random.normal(second_key, shape, jnp.float32), -4.0, 4.0)
    return (query_base, key_base)


def draw_queries(key, part):
    query_base, key_base = paired_draw(key)
    return query_base.astype(jnp.bfloat16)


def draw_keys(key, part):
    query_base, key_base = paired_draw(key)
    return key_base.astype(jnp.bfloat16)


def draw_values(key, part):
    base_key = jax.random.fold_in(key, 29)
    noise_key, amp_key, freq_key, phase_key = jax.random.split(base_key, 4)
    shape = (TOKENS, HEADS, HEAD_DIM)
    amplitude = jnp.exp(jax.random.uniform(amp_key, (HEADS, HEAD_DIM), jnp.float32, math.log(0.5), math.log(1.5)))
    frequency = jax.random.uniform(freq_key, (HEADS, HEAD_DIM), jnp.float32, 0.5, 3.0)
    phase = jax.random.uniform(phase_key, (HEADS, HEAD_DIM), jnp.float32, 0.0, 2.0 * math.pi)
    position = jnp.arange(TOKENS).astype(jnp.float32)[:, None, None] / TOKENS
    wave = jnp.cos(2.0 * math.pi * frequency[None] * position + phase[None])
    noise = jnp.clip(jax.random.normal(noise_key, shape, jnp.float32), -4.0, 4.0)
    drawn = noise + amplitude[None] * wave
    return drawn.astype(jnp.bfloat16)


def draw_feature_map(key, part):
    base_key = jax.random.fold_in(key, 41)
    main_key = jax.random.fold_in(base_key, 0)
    shape = (HEADS, HEAD_DIM, FEAT)
    normal_part = jnp.clip(jax.random.normal(main_key, shape, jnp.float32), -4.0, 4.0)
    drawn = normal_part * HEAD_DIM ** (-0.5)
    return drawn


def profile(amount, total, bound, lean):
    loads = [(1 << 20) // math.isqrt(standing ** lean) + 1 for standing in range(2, amount + 1)]
    surplus, counts = total - bound - (amount - 1), [1] * (amount - 1)
    while surplus > 0:
        free = [i for i in range(amount - 1) if counts[i] < bound]
        whole, remaining = sum([loads[i] for i in free]), surplus
        for i in free:
            more = min(bound - counts[i], max(1, remaining * loads[i] // whole), surplus)
            counts[i] = counts[i] + more
            surplus = surplus - more
    return np.array([bound] + counts)


def ragged_sizes(own_key, number_of, total, limit, skew):
    if number_of == 2:
        one = jax.random.randint(own_key, (), max(1, total - limit), min(limit, total - 1) + 1)
        return jnp.stack([one, total - one])
    tallies = jnp.asarray(profile(number_of, total, limit, skew), jnp.int32)
    pairs = (number_of - 1) // 2
    donor, receiver = tallies[1:1 + 2 * pairs:2], tallies[2:2 + 2 * pairs:2]
    room = jnp.minimum(donor - 1, limit - receiver)
    moved = jax.random.randint(jax.random.fold_in(own_key, 1), (pairs,), 0, 1 << 20) % (room + 1)
    tallies = tallies.at[1:1 + 2 * pairs:2].set(donor - moved).at[2:2 + 2 * pairs:2].set(receiver + moved)
    return tallies[jax.random.permutation(jax.random.fold_in(own_key, 2), number_of)]


def setup_inputs(seed: int = 0) -> dict:
    key_of = jax.random.split(jax.random.key(seed), 6)
    return {
        "queries": draw_queries(jax.random.fold_in(key_of[5], 71), 0),
        "keys": draw_keys(jax.random.fold_in(key_of[5], 71), 0),
        "values": draw_values(jax.random.fold_in(key_of[5], 71), 0),
        "documents": jnp.searchsorted(jnp.cumsum(ragged_sizes(key_of[3], DOCS, TOKENS, DOC_MOST, 1)), jnp.arange(TOKENS), side="right").astype(jnp.int32),
        "feature_map": draw_feature_map(jax.random.fold_in(key_of[5], 71), 0),
    }


exact_mode = lax.Precision.HIGHEST
masked_value = -1e+30

def features(inputs, weights):
    logits = jnp.einsum('rhd,hdf->rhf', inputs, weights, precision=exact_mode)
    return jnp.concatenate([jax.nn.softmax(logits, axis=-1), jax.nn.softmax(-logits, axis=-1)], axis=-1)

def join_up(earlier, later):
    merged_tag = jnp.maximum(earlier[0], later[0])
    early_keep = (earlier[0] == merged_tag).astype(earlier[1].dtype)
    late_keep = (later[0] == merged_tag).astype(later[1].dtype)
    return (merged_tag, early_keep * earlier[1] + late_keep * later[1], early_keep * earlier[2] + late_keep * later[2])

def teacher(queries, keys, values, documents):
    position = jnp.arange(TOKENS)
    allowed = (position[None, :] <= position[:, None]) & (documents[None, :] == documents[:, None])
    score_scale = HEAD_DIM ** (-0.5)

    def one_head(operands):
        head_query, head_key, head_value = operands
        scores = jnp.dot(head_query.astype(jnp.float32), head_key.astype(jnp.float32).T, precision=exact_mode) * score_scale
        scores = jnp.where(allowed, scores, masked_value)
        row_max = lax.optimization_barrier(jnp.max(scores, axis=1, keepdims=True))
        probabilities = jnp.where(allowed, jnp.exp(scores - row_max), 0.0)
        totals = lax.optimization_barrier(jnp.sum(probabilities, axis=1, keepdims=True))
        rounded = lax.optimization_barrier(probabilities.astype(jnp.bfloat16)).astype(jnp.float32)
        numerator = jnp.dot(rounded, head_value.astype(jnp.float32), precision=exact_mode)
        return (numerator / totals).astype(jnp.bfloat16)
    per_head = lax.map(one_head, (jnp.swapaxes(queries, 0, 1), jnp.swapaxes(keys, 0, 1), jnp.swapaxes(values, 0, 1)))
    return jnp.swapaxes(per_head, 0, 1)

def student(queries, keys, values, documents, weights):
    half_feat = FEAT // 2
    score_scale = HEAD_DIM ** (-0.5)
    query_float = queries.astype(jnp.float32)
    key_float = keys.astype(jnp.float32)
    value_float = values.astype(jnp.float32)
    query_feat = features(query_float, weights[:, :, :half_feat])
    key_feat = features(key_float, weights[:, :, half_feat:])
    block_count = TOKENS // WINDOW
    doc_float = documents.astype(jnp.float32)

    def padded(array, filler):
        front = jnp.full((WINDOW,) + array.shape[1:], filler, array.dtype)
        return jnp.concatenate([front, array], axis=0).reshape((block_count + 1, WINDOW) + array.shape[1:])

    def paired(blocks):
        return jnp.concatenate([blocks[:-1], blocks[1:]], axis=1)
    key_blocks = padded(key_float, 0.0)
    value_blocks = padded(value_float, 0.0)
    feat_blocks = padded(key_feat, 0.0)
    doc_blocks = padded(doc_float, -1.0)
    inputs_all = (query_float.reshape(block_count, WINDOW, HEADS, HEAD_DIM), query_feat.reshape(block_count, WINDOW, HEADS, FEAT), doc_float.reshape(block_count, WINDOW), paired(key_blocks), paired(value_blocks), paired(feat_blocks), paired(doc_blocks), value_blocks[:-1], feat_blocks[:-1], doc_blocks[:-1])
    distance = jnp.arange(WINDOW)[:, None] + WINDOW - jnp.arange(2 * WINDOW)[None, :]
    in_window = (distance >= 0) & (distance < WINDOW)
    beyond = distance >= WINDOW

    def block_step(carried, block_inputs):
        tag_in, state_in, norm_in = carried
        block_query, block_qfeat, block_docs, near_keys, near_values, near_feat, near_docs, elem_values, elem_feat, elem_docs = block_inputs
        same_doc = block_docs[:, None] == near_docs[None, :]
        scores = jnp.einsum('ihd,jhd->hij', block_query, near_keys, precision=exact_mode) * score_scale
        window_mask = (in_window & same_doc)[None]
        row_max = lax.optimization_barrier(jnp.max(jnp.where(window_mask, scores, masked_value), axis=-1, keepdims=True))
        window_weight = jnp.where(window_mask, jnp.exp(scores - row_max), 0.0)
        linear_weight = jnp.where((beyond & same_doc)[None], jnp.einsum('ihf,jhf->hij', block_qfeat, near_feat, precision=exact_mode), 0.0)
        weight = window_weight + linear_weight
        uses_state = (block_docs == tag_in).astype(jnp.float32)[:, None]
        numer_sum = jnp.einsum('hij,jhd->ihd', weight, near_values, precision=exact_mode)
        numer_sum = numer_sum + uses_state[:, :, None] * jnp.einsum('ihf,hfd->ihd', block_qfeat, state_in, precision=exact_mode)
        denominator = lax.optimization_barrier(jnp.sum(weight, axis=-1)).T + uses_state * jnp.einsum('ihf,hf->ih', block_qfeat, norm_in, precision=exact_mode)
        output = numer_sum / denominator[:, :, None]
        elem_tag = elem_docs[-1]
        in_tail = (elem_docs == elem_tag).astype(jnp.float32)
        masked_feat = elem_feat * in_tail[:, None, None]
        elem_state = jnp.einsum('jhf,jhd->hfd', masked_feat, elem_values, precision=exact_mode)
        elem_norm = lax.optimization_barrier(jnp.sum(masked_feat, axis=0))
        return (join_up(carried, (elem_tag, elem_state, elem_norm)), output)
    start_carry = (jnp.float32(-2.0), jnp.zeros((HEADS, FEAT, HEAD_DIM), jnp.float32), jnp.zeros((HEADS, FEAT), jnp.float32))
    final_carry, outputs = lax.scan(block_step, start_carry, inputs_all)
    return outputs.reshape(TOKENS, HEADS, HEAD_DIM)

def reference(queries, keys, values, documents, feature_map):
    teacher_out = teacher(queries, keys, values, documents)
    target = teacher_out.astype(jnp.float32)

    def objective(weights):
        output = student(queries, keys, values, documents, weights)
        loss_total = jnp.sum(jnp.square(output - target)) / (TOKENS * HEADS)
        return (loss_total, output)
    (loss_total, output), feature_grad = jax.value_and_grad(objective, has_aux=True)(feature_map)
    return (teacher_out, output.astype(jnp.bfloat16), loss_total, feature_grad)
```

```python
import functools
import math

import jax
import jax.numpy as jnp
from jax import lax
from jax.experimental import pallas as pl
from jax.experimental.pallas import tpu as pltpu
from jax.sharding import PartitionSpec as P

WINDOW = 64
DOC_VALUES = 4
LANES = 128
META_ROWS = 16
BLOCK = 256
LOG2E = math.log2(math.e)


exact_mode = lax.Precision.HIGHEST
masked_value = -1e30


def passed_along(block, axis, distance):
    devices = range(lax.axis_size(axis))
    route = [(i - distance, i) for i in devices if i - distance in devices]
    return lax.ppermute(block, axis, route)


def features(inputs, weights):
    logits = jnp.einsum("rhd,hdf->rhf", inputs, weights, precision=exact_mode)
    return jnp.concatenate(
        [jax.nn.softmax(logits, axis=-1), jax.nn.softmax(-logits, axis=-1)], axis=-1
    )


def join_up(earlier, later):
    merged_tag = jnp.maximum(earlier[0], later[0])
    early_keep = (earlier[0] == merged_tag).astype(earlier[1].dtype)
    late_keep = (later[0] == merged_tag).astype(later[1].dtype)
    return (
        merged_tag,
        early_keep * earlier[1] + late_keep * later[1],
        early_keep * earlier[2] + late_keep * later[2],
    )


def join_down(earlier, later):
    merged_tag = jnp.minimum(earlier[0], later[0])
    early_keep = (earlier[0] == merged_tag).astype(earlier[1].dtype)
    late_keep = (later[0] == merged_tag).astype(later[1].dtype)
    return (
        merged_tag,
        early_keep * earlier[1] + late_keep * later[1],
        early_keep * earlier[2] + late_keep * later[2],
    )


def relay_body(queries, keys, values, documents, feature_map):
    tok_rows, head_count, head_width = queries.shape
    half_feat = feature_map.shape[2] // 2
    score_scale = head_width ** (-0.5)
    seq_place = lax.axis_index("seq")
    seq_count = lax.axis_size("seq")
    first_row = seq_place * tok_rows
    doc_float = documents.astype(jnp.float32)
    doc_marks = (documents + 1).astype(jnp.bfloat16)
    query_pos = first_row + jnp.arange(tok_rows)

    def attend(carried, portion):
        key_piece, value_piece, mark_piece = portion
        key_pos = jnp.arange(key_piece.shape[0])
        same_doc = mark_piece.astype(jnp.float32)[None, :] - 1.0 == doc_float[:, None]
        allowed = (same_doc & (key_pos[None, :] <= query_pos[:, None]))[:, None, :]
        scores = (
            jnp.einsum("ihd,jhd->ihj", queries, key_piece, preferred_element_type=jnp.float32)
            * score_scale
        )
        scores = jnp.where(allowed, scores, masked_value)
        row_max, totals, numerator = carried
        new_max = jnp.maximum(row_max, jnp.max(scores, axis=-1))
        probabilities = jnp.where(allowed, jnp.exp(scores - new_max[:, :, None]), 0.0)
        totals = jnp.sum(probabilities, axis=-1)
        numerator = jnp.einsum(
            "ihj,jhd->ihd",
            probabilities.astype(jnp.bfloat16),
            value_piece,
            preferred_element_type=jnp.float32,
        )
        return (new_max, totals, numerator)

    start_carry = (
        jnp.full((tok_rows, head_count), masked_value, jnp.float32),
        jnp.zeros((tok_rows, head_count), jnp.float32),
        jnp.zeros((tok_rows, head_count, head_width), jnp.float32),
    )
    portion = (
        lax.all_gather(keys, "seq", axis=0, tiled=True),
        lax.all_gather(values, "seq", axis=0, tiled=True),
        lax.all_gather(doc_marks, "seq", axis=0, tiled=True),
    )
    touches = (jnp.int32(0) < first_row + tok_rows) & (
        portion[2][-1].astype(jnp.float32) - 1.0 >= doc_float[0]
    )

    def compute_update(held_carry):
        return attend(held_carry, portion)

    def keep_carry(held_carry):
        return held_carry

    row_max, totals, numerator = lax.cond(touches, compute_update, keep_carry, start_carry)
    teacher_out = (numerator / totals[:, :, None]).astype(jnp.bfloat16)
    target = teacher_out.astype(jnp.float32)
    halo_keys, halo_values, halo_marks = passed_along(
        (keys[tok_rows - WINDOW :], values[tok_rows - WINDOW :], doc_marks[tok_rows - WINDOW :]),
        "seq",
        1,
    )
    key_joined = jnp.concatenate([halo_keys, keys], axis=0)
    key_float = key_joined.astype(jnp.float32)
    value_float = jnp.concatenate([halo_values, values], axis=0).astype(jnp.float32)
    doc_all = jnp.concatenate([halo_marks.astype(jnp.float32) - 1.0, doc_float], axis=0)
    query_float = queries.astype(jnp.float32)
    distance = jnp.arange(tok_rows)[:, None] + WINDOW - jnp.arange(tok_rows + WINDOW)[None, :]
    same_doc = doc_float[:, None] == doc_all[None, :]
    in_window = same_doc & (distance >= 0) & (distance < WINDOW)
    beyond = same_doc & (distance >= WINDOW)
    scores = (
        jnp.einsum("ihd,jhd->hij", queries, key_joined, preferred_element_type=jnp.float32)
        * score_scale
    )
    window_row = jnp.max(jnp.where(in_window[None], scores, masked_value), axis=-1, keepdims=True)
    window_weight = jnp.where(in_window[None], jnp.exp(scores - window_row), 0.0)
    elem_keys = key_float[:tok_rows]
    elem_values = value_float[:tok_rows]
    elem_docs = doc_all[:tok_rows]
    elem_tag = elem_docs[tok_rows - 1]
    in_tail = (elem_docs == elem_tag).astype(jnp.float32)

    def element(weights):
        masked_feat = features(elem_keys, weights[:, :, half_feat:]) * in_tail[:, None, None]
        return (
            jnp.einsum("jhf,jhd->hfd", masked_feat, elem_values, precision=exact_mode),
            jnp.sum(masked_feat, axis=0),
        )

    (elem_state, elem_norm), element_pullback = jax.vjp(element, feature_map)
    blank_state = jnp.zeros_like(elem_state)
    blank_norm = jnp.zeros_like(elem_norm)
    forward_blank = (jnp.float32(-2.0), blank_state, blank_norm)

    def relay_step(turn_index, carried):
        arrived = passed_along(join_up(carried, (elem_tag, elem_state, elem_norm)), "seq", 1)
        return jax.tree.map(
            lambda received, blank_entry: jnp.where(seq_place == 0, blank_entry, received),
            arrived,
            forward_blank,
        )

    tag_in, state_in, norm_in = lax.fori_loop(0, seq_count - 1, relay_step, forward_blank)
    uses_state = (doc_float == tag_in).astype(jnp.float32)[:, None]
    normaliser = 1.0 / (tok_rows * seq_count * head_count * lax.axis_size(("grp", "head")))

    def local_loss(weights, state, norm):
        query_feat = features(query_float, weights[:, :, :half_feat])
        key_feat = features(key_float, weights[:, :, half_feat:])
        linear = jnp.where(
            beyond[None],
            jnp.einsum("ihf,jhf->hij", query_feat, key_feat, precision=exact_mode),
            0.0,
        )
        weight = window_weight + linear
        numer_sum = jnp.einsum("hij,jhd->ihd", weight, value_float, precision=exact_mode)
        numer_sum = numer_sum + uses_state[:, :, None] * jnp.einsum(
            "ihf,hfd->ihd", query_feat, state, precision=exact_mode
        )
        denominator = jnp.sum(weight, axis=-1).T + uses_state * jnp.einsum(
            "ihf,hf->ih", query_feat, norm, precision=exact_mode
        )
        output = numer_sum / denominator[:, :, None]
        return (jnp.sum(jnp.square(output - target)) * normaliser, output)

    local_part, local_pullback, output = jax.vjp(
        local_loss, feature_map, state_in, norm_in, has_aux=True
    )
    grad_direct, grad_state, grad_norm = local_pullback(jnp.ones_like(local_part))
    backward_blank = (jnp.float32(1000000000.0), blank_state, blank_norm)

    def return_step(turn_index, carried):
        arrived = passed_along(join_down(carried, (tag_in, grad_state, grad_norm)), "seq", -1)
        return jax.tree.map(
            lambda received, blank_entry: jnp.where(
                seq_place == seq_count - 1, blank_entry, received
            ),
            arrived,
            backward_blank,
        )

    back_tag, carried_state, carried_norm = lax.fori_loop(
        0, seq_count - 1, return_step, backward_blank
    )
    total_grad = grad_direct + element_pullback((carried_state, carried_norm))[0]
    feature_grad = lax.psum(total_grad, "seq")
    loss_total = lax.psum(local_part, ("grp", "seq", "head"))
    return (teacher_out, output.astype(jnp.bfloat16), loss_total, feature_grad)


def turned(block, axis, distance):
    count = lax.axis_size(axis)
    return lax.ppermute(block, axis, [(i, (i + distance) % count) for i in range(count)])


def crossed(block, axis, mask):
    count = lax.axis_size(axis)
    return lax.ppermute(block, axis, [(i, i ^ mask) for i in range(count)])


def summed_over(block, axis):
    count = lax.axis_size(axis)
    if count == 1:
        return block
    if count == 2:
        return block + crossed(block, axis, 1)
    if count == 4:
        return (block + crossed(block, axis, 2)) + (
            crossed(block, axis, 1) + crossed(block, axis, 3)
        )
    return lax.psum(block, axis)


def fits_split(tok_rows, head_count, head_width, feat, seq_count):
    return (
        head_count % seq_count == 0
        and head_count % 8 == 0
        and tok_rows % 16 == 0
        and tok_rows <= 256
        and tok_rows * seq_count <= 1536
        and (tok_rows * seq_count) % BLOCK == 0
        and head_width == LANES
        and feat == LANES
    )


def dot_nn(a, b):
    return jnp.dot(a, b, preferred_element_type=jnp.float32)


def dot_nt(a, b):
    return lax.dot_general(a, b, (((1,), (1,)), ((), ())), preferred_element_type=jnp.float32)


def dot_tn(a, b):
    return lax.dot_general(a, b, (((0,), (0,)), ((), ())), preferred_element_type=jnp.float32)


def place_of(shift, seq_count):
    return lax.rem(lax.axis_index("seq") + (seq_count - shift), seq_count)


def pack_kernel(seq_count, per_place, chunk, q_ref, k_ref, v_ref, doc_ref, *rest):
    outs, wide = rest[:seq_count], rest[seq_count]
    rows = doc_ref.shape[1]
    heads = seq_count * per_place
    docs = doc_ref[...]
    meta_row = lax.broadcasted_iota(jnp.int32, (META_ROWS, LANES), 0)
    meta = jnp.zeros((META_ROWS, LANES), jnp.float32)
    for value in range(DOC_VALUES - 1):
        amount = jnp.sum((docs <= value).astype(jnp.float32), axis=1, keepdims=True)
        meta = jnp.where(meta_row == value, amount, meta)
    for n, ref in enumerate((q_ref, k_ref, v_ref)):
        wide[n] = ref[...].astype(jnp.float32)
    for shift, out in enumerate(outs):
        head = lax.rem(lax.axis_index("seq") + shift, seq_count) * per_place + chunk
        for n in range(3):
            out[n * rows : (n + 1) * rows, :] = wide[
                n, pl.ds(head, rows, stride=heads), :
            ].astype(jnp.bfloat16)
        out[3 * rows :, :] = meta.astype(jnp.bfloat16)


def half_sums(array, ones_block):
    high = array.astype(jnp.bfloat16)
    low = (array - high.astype(jnp.float32)).astype(jnp.bfloat16)
    return dot_nn(high, ones_block) + dot_nn(low, ones_block)


def signed_features(inputs, weights, ones_block, left):
    first = weights.astype(jnp.bfloat16)
    left_over = weights - first.astype(jnp.float32)
    second = left_over.astype(jnp.bfloat16)
    third = (left_over - second.astype(jnp.float32)).astype(jnp.bfloat16)
    logits = dot_nn(inputs, first) + dot_nn(inputs, second) + dot_nn(inputs, third)
    left_most = jnp.max(jnp.where(left, logits, -jnp.inf), axis=1, keepdims=True)
    right_most = jnp.max(jnp.where(left, -jnp.inf, logits), axis=1, keepdims=True)
    raised = jnp.exp2((logits - jnp.where(left, left_most, right_most)) * LOG2E)
    return raised / half_sums(raised, ones_block)


def head_kernel(seq_count, per_place, chunk, score_scale, normaliser, *refs):
    pieces, map_ref = refs[:seq_count], refs[seq_count]
    outs = refs[seq_count + 1 : 2 * seq_count + 1]
    loss_ref = refs[2 * seq_count + 1]
    q_s, k_s, v_s, t_s, s_s, qf_s, kf_s, qb_s, kb_s, dq_s, dk_s = refs[2 * seq_count + 2 :]
    total = q_s.shape[0]
    rows = total // seq_count
    exponent = score_scale * LOG2E

    counts = jnp.zeros((META_ROWS, LANES), jnp.float32)
    for shift, piece in enumerate(pieces):
        first = pl.multiple_of(place_of(shift, seq_count) * rows, 16)
        q_s[pl.ds(first, rows), :] = piece[:rows, :]
        k_s[pl.ds(first, rows), :] = piece[rows : 2 * rows, :]
        v_s[pl.ds(first, rows), :LANES] = piece[2 * rows : 3 * rows, :]
        counts = counts + piece[3 * rows :, :].astype(jnp.float32)
    v_s[:, LANES:] = jnp.ones((total, LANES), jnp.bfloat16)
    bounds = counts.astype(jnp.int32)

    lane = lax.broadcasted_iota(jnp.int32, (1, LANES), 1)
    left = lane < LANES // 2
    block_row = lax.broadcasted_iota(jnp.int32, (LANES, LANES), 0)
    block_col = lax.broadcasted_iota(jnp.int32, (LANES, LANES), 1)
    ones_block = ((block_row < LANES // 2) == (block_col < LANES // 2)).astype(jnp.bfloat16)

    weights = map_ref[lax.axis_index("seq") * per_place + chunk]
    rolled = pltpu.roll(weights, LANES // 2, 1)
    q_feat = signed_features(q_s[...], jnp.where(left, weights, -rolled), ones_block, left)
    k_feat = signed_features(k_s[...], jnp.where(left, rolled, -weights), ones_block, left)
    qf_s[...] = q_feat
    kf_s[...] = k_feat
    qb_s[...] = q_feat.astype(jnp.bfloat16)
    kb_s[...] = k_feat.astype(jnp.bfloat16)
    dk_s[...] = jnp.zeros_like(dk_s)
    loss = jnp.zeros((8, LANES), jnp.float32)

    for first in range(0, total, BLOCK):
        last = first + BLOCK
        near = max(0, first - LANES)
        place = lax.broadcasted_iota(jnp.int32, (BLOCK, LANES), 0) + first
        start = jnp.zeros((BLOCK, LANES), jnp.int32)
        for value in range(DOC_VALUES - 1):
            bound = bounds[value : value + 1, :]
            start = jnp.maximum(start, jnp.where(bound <= place, bound, 0))
        row = place[:, :1]
        col = lax.broadcasted_iota(jnp.int32, (BLOCK, last), 1)
        visible = (col <= row) & (col >= start[:, :1])
        far = (col <= row - WINDOW) & (col >= start[:, :1])
        window = visible[:, near:] & (col[:, near:] > row - WINDOW)
        scores = dot_nt(q_s[first:last, :], k_s[:last, :])
        shown = jnp.where(visible, scores, masked_value)
        raised = jnp.exp2((shown - jnp.max(shown, axis=1, keepdims=True)) * exponent)
        numer = dot_nn(raised.astype(jnp.bfloat16), v_s[:last, :LANES])
        teacher = (numer / jnp.sum(raised, axis=1, keepdims=True)).astype(jnp.bfloat16)
        t_s[first:last, :] = teacher

        shown = jnp.where(window, scores[:, near:], masked_value)
        raised = jnp.exp2((shown - jnp.max(shown, axis=1, keepdims=True)) * exponent)
        linear = dot_nt(qb_s[first:last, :], kb_s[:last, :])
        weight = jnp.where(far[:, near:], linear[:, near:], raised)
        if near:
            weight = jnp.concatenate(
                [jnp.where(far[:, :near], linear[:, :near], 0.0), weight], axis=1
            )
        sums = dot_nn(weight.astype(jnp.bfloat16), v_s[:last, :])
        inverse = 1.0 / sums[:, LANES:]
        output = sums[:, :LANES] * inverse
        s_s[first:last, :] = output.astype(jnp.bfloat16)
        error = output - teacher.astype(jnp.float32)
        loss = loss + jnp.sum((error * error).reshape(BLOCK // 8, 8, LANES), axis=0)

        slope = error * (2.0 * normaliser)
        slope_numer = slope * inverse
        slope_denom = -jnp.sum(slope * output, axis=1, keepdims=True) * inverse
        high = slope_denom.astype(jnp.bfloat16).astype(jnp.float32)
        extra = jnp.where(lane == 0, high, jnp.where(lane == 1, slope_denom - high, 0.0))
        slopes = jnp.concatenate(
            [slope_numer.astype(jnp.bfloat16), extra.astype(jnp.bfloat16)], axis=1
        )
        slope_weight = jnp.where(far, dot_nt(slopes, v_s[:last, :]), 0.0).astype(jnp.bfloat16)
        dq_s[first:last, :] = dot_nn(slope_weight, kb_s[:last, :])
        dk_s[:last, :] += dot_tn(slope_weight, qb_s[first:last, :])

    def logits_slope(feat, slope):
        product = feat * slope
        return (product - feat * half_sums(product, ones_block)).astype(jnp.bfloat16)

    from_q = dot_tn(q_s[...], logits_slope(qf_s[...], dq_s[...]))
    from_k = dot_tn(k_s[...], logits_slope(kf_s[...], dk_s[...]))
    grad = jnp.where(
        left,
        from_q - pltpu.roll(from_q, LANES // 2, 1),
        pltpu.roll(from_k, LANES // 2, 1) - from_k,
    ).astype(jnp.bfloat16)
    for shift, out in enumerate(outs):
        first = lax.rem(lax.axis_index("seq") + shift, seq_count) * rows
        first = pl.multiple_of(first, 16)
        out[:rows, :] = t_s[pl.ds(first, rows), :]
        out[rows : 2 * rows, :] = s_s[pl.ds(first, rows), :]
        out[2 * rows :, :] = grad
    loss_ref[...] = loss * normaliser


def unpack_kernel(seq_count, per_place, *refs):
    pieces = refs[: seq_count * per_place]
    t_ref, s_ref, grad_ref, t_wide, s_wide = refs[seq_count * per_place :]
    heads = seq_count * per_place
    rows = t_ref.shape[0] // heads
    for chunk in range(per_place):
        for shift in range(seq_count):
            piece = pieces[chunk * seq_count + shift]
            head = place_of(shift, seq_count) * per_place + chunk
            t_wide[pl.ds(head, rows, stride=heads), :] = piece[:rows, :].astype(jnp.float32)
            s_wide[pl.ds(head, rows, stride=heads), :] = piece[rows : 2 * rows, :].astype(
                jnp.float32
            )
            grad_ref[head] = piece[2 * rows :, :].astype(jnp.float32)
    t_ref[...] = t_wide[...].astype(jnp.bfloat16)
    s_ref[...] = s_wide[...].astype(jnp.bfloat16)


def kernel_call(kernel, out_shape, scratch_shapes, flops, moved, name):
    return pl.pallas_call(
        kernel,
        out_shape=out_shape,
        scratch_shapes=scratch_shapes,
        compiler_params=pltpu.CompilerParams(vmem_limit_bytes=48 * 1024 * 1024),
        cost_estimate=pl.CostEstimate(flops=flops, bytes_accessed=moved, transcendentals=0),
        name=name,
    )


def split_body(queries, keys, values, documents, feature_map):
    tok_rows, head_count, head_width = queries.shape
    seq_count = lax.axis_size("seq")
    per_place = head_count // seq_count
    total = tok_rows * seq_count
    score_scale = head_width ** (-0.5)
    normaliser = 1.0 / (total * head_count * lax.axis_size(("grp", "head")))
    flat = [a.reshape(tok_rows * head_count, head_width) for a in (queries, keys, values)]
    docs = documents.reshape(1, tok_rows)
    sent_rows = 3 * tok_rows + META_ROWS
    back_rows = 2 * tok_rows + head_width
    bf16, f32 = jnp.bfloat16, jnp.float32

    held = []
    for chunk in range(per_place):
        packed = kernel_call(
            functools.partial(pack_kernel, seq_count, per_place, chunk),
            [jax.ShapeDtypeStruct((sent_rows, LANES), bf16)] * seq_count,
            [pltpu.VMEM((3, tok_rows * head_count, LANES), f32)],
            0,
            12 * tok_rows * head_count * LANES,
            "pack",
        )(*flat, docs)
        held.append(
            [packed[0]] + [turned(packed[d], "seq", d) for d in range(1, seq_count)]
        )

    returned = []
    loss = jnp.zeros((8, LANES), f32)
    for chunk in range(per_place):
        *packed, part = kernel_call(
            functools.partial(
                head_kernel, seq_count, per_place, chunk, score_scale, normaliser
            ),
            [jax.ShapeDtypeStruct((back_rows, LANES), bf16)] * seq_count
            + [jax.ShapeDtypeStruct((8, LANES), f32)],
            [
                pltpu.VMEM((total, LANES), bf16),
                pltpu.VMEM((total, LANES), bf16),
                pltpu.VMEM((total, 2 * LANES), bf16),
                pltpu.VMEM((total, LANES), bf16),
                pltpu.VMEM((total, LANES), bf16),
                pltpu.VMEM((total, LANES), f32),
                pltpu.VMEM((total, LANES), f32),
                pltpu.VMEM((total, LANES), bf16),
                pltpu.VMEM((total, LANES), bf16),
                pltpu.VMEM((total, LANES), f32),
                pltpu.VMEM((total, LANES), f32),
            ],
            14 * total * total * LANES,
            16 * total * LANES,
            "one_head",
        )(*held[chunk], feature_map)
        returned += [packed[0]] + [turned(packed[d], "seq", d) for d in range(1, seq_count)]
        loss = loss + part

    loss = jnp.full((8, LANES), jnp.sum(loss), f32)
    for axis in ("grp", "head", "seq"):
        loss = summed_over(loss, axis)
    teacher_out, student_out, feature_grad = kernel_call(
        functools.partial(unpack_kernel, seq_count, per_place),
        [
            jax.ShapeDtypeStruct((tok_rows * head_count, LANES), bf16),
            jax.ShapeDtypeStruct((tok_rows * head_count, LANES), bf16),
            jax.ShapeDtypeStruct(feature_map.shape, f32),
        ],
        [pltpu.VMEM((tok_rows * head_count, LANES), f32)] * 2,
        0,
        12 * tok_rows * head_count * LANES,
        "unpack",
    )(*returned)
    return (
        teacher_out.reshape(queries.shape),
        student_out.reshape(queries.shape),
        loss[0, 0],
        feature_grad,
    )


def body(queries, keys, values, documents, feature_map):
    tok_rows, head_count, head_width = queries.shape
    if fits_split(tok_rows, head_count, head_width, feature_map.shape[2], lax.axis_size("seq")):
        return split_body(queries, keys, values, documents, feature_map)
    return relay_body(queries, keys, values, documents, feature_map)


def solution(mesh):
    in_specs = (
        P("seq", ("grp", "head"), None),
        P("seq", ("grp", "head"), None),
        P("seq", ("grp", "head"), None),
        P("seq"),
        P(("grp", "head"), None, None),
    )
    out_specs = (
        P("seq", ("grp", "head"), None),
        P("seq", ("grp", "head"), None),
        P(),
        P(("grp", "head"), None, None),
    )
    return jax.shard_map(body, mesh=mesh, in_specs=in_specs, out_specs=out_specs, check_vma=False)
```

```python
import functools
import math

import jax
import jax.numpy as jnp
from jax import lax
from jax.experimental import pallas as pl
from jax.experimental.pallas import tpu as pltpu
from jax.sharding import PartitionSpec as P

WINDOW = 64
DOC_VALUES = 4
LANES = 128
META_ROWS = 16
BLOCK = 256
LOG2E = math.log2(math.e)
COPIES = 4

PACK_VMEM = 62
HEAD_COST = 6_000_000_000


exact_mode = lax.Precision.HIGHEST
masked_value = -1e30


def passed_along(block, axis, distance):
    devices = range(lax.axis_size(axis))
    route = [(i - distance, i) for i in devices if i - distance in devices]
    return lax.ppermute(block, axis, route)


def features(inputs, weights):
    logits = jnp.einsum("rhd,hdf->rhf", inputs, weights, precision=exact_mode)
    return jnp.concatenate(
        [jax.nn.softmax(logits, axis=-1), jax.nn.softmax(-logits, axis=-1)], axis=-1
    )


def join_up(earlier, later):
    merged_tag = jnp.maximum(earlier[0], later[0])
    early_keep = (earlier[0] == merged_tag).astype(earlier[1].dtype)
    late_keep = (later[0] == merged_tag).astype(later[1].dtype)
    return (
        merged_tag,
        early_keep * earlier[1] + late_keep * later[1],
        early_keep * earlier[2] + late_keep * later[2],
    )


def join_down(earlier, later):
    merged_tag = jnp.minimum(earlier[0], later[0])
    early_keep = (earlier[0] == merged_tag).astype(earlier[1].dtype)
    late_keep = (later[0] == merged_tag).astype(later[1].dtype)
    return (
        merged_tag,
        early_keep * earlier[1] + late_keep * later[1],
        early_keep * earlier[2] + late_keep * later[2],
    )


def relay_body(queries, keys, values, documents, feature_map):
    tok_rows, head_count, head_width = queries.shape
    half_feat = feature_map.shape[2] // 2
    score_scale = head_width ** (-0.5)
    seq_place = lax.axis_index("seq")
    seq_count = lax.axis_size("seq")
    first_row = seq_place * tok_rows
    doc_float = documents.astype(jnp.float32)
    doc_marks = (documents + 1).astype(jnp.bfloat16)
    query_pos = first_row + jnp.arange(tok_rows)

    def attend(carried, portion):
        key_piece, value_piece, mark_piece = portion
        key_pos = jnp.arange(key_piece.shape[0])
        same_doc = mark_piece.astype(jnp.float32)[None, :] - 1.0 == doc_float[:, None]
        allowed = (same_doc & (key_pos[None, :] <= query_pos[:, None]))[:, None, :]
        scores = (
            jnp.einsum("ihd,jhd->ihj", queries, key_piece, preferred_element_type=jnp.float32)
            * score_scale
        )
        scores = jnp.where(allowed, scores, masked_value)
        row_max, totals, numerator = carried
        new_max = jnp.maximum(row_max, jnp.max(scores, axis=-1))
        probabilities = jnp.where(allowed, jnp.exp(scores - new_max[:, :, None]), 0.0)
        totals = jnp.sum(probabilities, axis=-1)
        numerator = jnp.einsum(
            "ihj,jhd->ihd",
            probabilities.astype(jnp.bfloat16),
            value_piece,
            preferred_element_type=jnp.float32,
        )
        return (new_max, totals, numerator)

    start_carry = (
        jnp.full((tok_rows, head_count), masked_value, jnp.float32),
        jnp.zeros((tok_rows, head_count), jnp.float32),
        jnp.zeros((tok_rows, head_count, head_width), jnp.float32),
    )
    portion = (
        lax.all_gather(keys, "seq", axis=0, tiled=True),
        lax.all_gather(values, "seq", axis=0, tiled=True),
        lax.all_gather(doc_marks, "seq", axis=0, tiled=True),
    )
    touches = (jnp.int32(0) < first_row + tok_rows) & (
        portion[2][-1].astype(jnp.float32) - 1.0 >= doc_float[0]
    )

    def compute_update(held_carry):
        return attend(held_carry, portion)

    def keep_carry(held_carry):
        return held_carry

    row_max, totals, numerator = lax.cond(touches, compute_update, keep_carry, start_carry)
    teacher_out = (numerator / totals[:, :, None]).astype(jnp.bfloat16)
    target = teacher_out.astype(jnp.float32)
    halo_keys, halo_values, halo_marks = passed_along(
        (keys[tok_rows - WINDOW :], values[tok_rows - WINDOW :], doc_marks[tok_rows - WINDOW :]),
        "seq",
        1,
    )
    key_joined = jnp.concatenate([halo_keys, keys], axis=0)
    key_float = key_joined.astype(jnp.float32)
    value_float = jnp.concatenate([halo_values, values], axis=0).astype(jnp.float32)
    doc_all = jnp.concatenate([halo_marks.astype(jnp.float32) - 1.0, doc_float], axis=0)
    query_float = queries.astype(jnp.float32)
    distance = jnp.arange(tok_rows)[:, None] + WINDOW - jnp.arange(tok_rows + WINDOW)[None, :]
    same_doc = doc_float[:, None] == doc_all[None, :]
    in_window = same_doc & (distance >= 0) & (distance < WINDOW)
    beyond = same_doc & (distance >= WINDOW)
    scores = (
        jnp.einsum("ihd,jhd->hij", queries, key_joined, preferred_element_type=jnp.float32)
        * score_scale
    )
    window_row = jnp.max(jnp.where(in_window[None], scores, masked_value), axis=-1, keepdims=True)
    window_weight = jnp.where(in_window[None], jnp.exp(scores - window_row), 0.0)
    elem_keys = key_float[:tok_rows]
    elem_values = value_float[:tok_rows]
    elem_docs = doc_all[:tok_rows]
    elem_tag = elem_docs[tok_rows - 1]
    in_tail = (elem_docs == elem_tag).astype(jnp.float32)

    def element(weights):
        masked_feat = features(elem_keys, weights[:, :, half_feat:]) * in_tail[:, None, None]
        return (
            jnp.einsum("jhf,jhd->hfd", masked_feat, elem_values, precision=exact_mode),
            jnp.sum(masked_feat, axis=0),
        )

    (elem_state, elem_norm), element_pullback = jax.vjp(element, feature_map)
    blank_state = jnp.zeros_like(elem_state)
    blank_norm = jnp.zeros_like(elem_norm)
    forward_blank = (jnp.float32(-2.0), blank_state, blank_norm)

    def relay_step(turn_index, carried):
        arrived = passed_along(join_up(carried, (elem_tag, elem_state, elem_norm)), "seq", 1)
        return jax.tree.map(
            lambda received, blank_entry: jnp.where(seq_place == 0, blank_entry, received),
            arrived,
            forward_blank,
        )

    tag_in, state_in, norm_in = lax.fori_loop(0, seq_count - 1, relay_step, forward_blank)
    uses_state = (doc_float == tag_in).astype(jnp.float32)[:, None]
    normaliser = 1.0 / (tok_rows * seq_count * head_count * lax.axis_size(("grp", "head")))

    def local_loss(weights, state, norm):
        query_feat = features(query_float, weights[:, :, :half_feat])
        key_feat = features(key_float, weights[:, :, half_feat:])
        linear = jnp.where(
            beyond[None],
            jnp.einsum("ihf,jhf->hij", query_feat, key_feat, precision=exact_mode),
            0.0,
        )
        weight = window_weight + linear
        numer_sum = jnp.einsum("hij,jhd->ihd", weight, value_float, precision=exact_mode)
        numer_sum = numer_sum + uses_state[:, :, None] * jnp.einsum(
            "ihf,hfd->ihd", query_feat, state, precision=exact_mode
        )
        denominator = jnp.sum(weight, axis=-1).T + uses_state * jnp.einsum(
            "ihf,hf->ih", query_feat, norm, precision=exact_mode
        )
        output = numer_sum / denominator[:, :, None]
        return (jnp.sum(jnp.square(output - target)) * normaliser, output)

    local_part, local_pullback, output = jax.vjp(
        local_loss, feature_map, state_in, norm_in, has_aux=True
    )
    grad_direct, grad_state, grad_norm = local_pullback(jnp.ones_like(local_part))
    backward_blank = (jnp.float32(1000000000.0), blank_state, blank_norm)

    def return_step(turn_index, carried):
        arrived = passed_along(join_down(carried, (tag_in, grad_state, grad_norm)), "seq", -1)
        return jax.tree.map(
            lambda received, blank_entry: jnp.where(
                seq_place == seq_count - 1, blank_entry, received
            ),
            arrived,
            backward_blank,
        )

    back_tag, carried_state, carried_norm = lax.fori_loop(
        0, seq_count - 1, return_step, backward_blank
    )
    total_grad = grad_direct + element_pullback((carried_state, carried_norm))[0]
    feature_grad = lax.psum(total_grad, "seq")
    loss_total = lax.psum(local_part, ("grp", "seq", "head"))
    return (teacher_out, output.astype(jnp.bfloat16), loss_total, feature_grad)


def turned(block, axis, distance):
    count = lax.axis_size(axis)
    return lax.ppermute(block, axis, [(i, (i + distance) % count) for i in range(count)])


def crossed(block, axis, mask):
    count = lax.axis_size(axis)
    return lax.ppermute(block, axis, [(i, i ^ mask) for i in range(count)])


def summed_over(block, axis):
    count = lax.axis_size(axis)
    if count == 1:
        return block
    if count == 2:
        return block + crossed(block, axis, 1)
    if count == 4:
        return (block + crossed(block, axis, 2)) + (
            crossed(block, axis, 1) + crossed(block, axis, 3)
        )
    return lax.psum(block, axis)


def fits_split(tok_rows, head_count, head_width, feat, seq_count):
    return (
        head_count % seq_count == 0
        and head_count % 8 == 0
        and tok_rows % 16 == 0
        and tok_rows <= 256
        and tok_rows * seq_count <= 1536
        and (tok_rows * seq_count) % BLOCK == 0
        and head_width == LANES
        and feat == LANES
    )


def dot_nn(a, b):
    return jnp.dot(a, b, preferred_element_type=jnp.float32)


def dot_nt(a, b):
    return lax.dot_general(a, b, (((1,), (1,)), ((), ())), preferred_element_type=jnp.float32)


def dot_tn(a, b):
    return lax.dot_general(a, b, (((0,), (0,)), ((), ())), preferred_element_type=jnp.float32)


def place_of(shift, seq_count):
    return lax.rem(lax.axis_index("seq") + (seq_count - shift), seq_count)


def pack_kernel(seq_count, per_place, q_ref, k_ref, v_ref, map_ref, doc_ref, *rest):
    outs = rest[: seq_count * per_place]
    own_map, narrow, wide, sems = rest[seq_count * per_place :]
    rows = doc_ref.shape[1]
    heads = seq_count * per_place
    part = rows * heads // COPIES
    copies = []
    for n, ref in enumerate((q_ref, k_ref, v_ref)):
        for piece in range(COPIES):
            span = pl.ds(piece * part, part)
            copies.append(
                pltpu.make_async_copy(
                    ref.at[span, :], narrow.at[n, span, :], sems.at[n * COPIES + piece]
                )
            )
    own = pl.ds(lax.axis_index("seq") * per_place, per_place)
    copies.append(pltpu.make_async_copy(map_ref.at[own], own_map, sems.at[3 * COPIES]))
    for copy in copies:
        copy.start()
    docs = doc_ref[...]
    meta_row = lax.broadcasted_iota(jnp.int32, (META_ROWS, LANES), 0)
    meta = jnp.zeros((META_ROWS, LANES), jnp.float32)
    for value in range(DOC_VALUES - 1):
        amount = jnp.sum((docs <= value).astype(jnp.float32), axis=1, keepdims=True)
        meta = jnp.where(meta_row == value, amount, meta)
    for n in range(3):
        for piece in range(COPIES):
            copies[n * COPIES + piece].wait()
            span = pl.ds(piece * part, part)
            wide[n, span, :] = narrow[n, span, :].astype(jnp.float32)
    for chunk in range(per_place):
        for shift in range(seq_count):
            out = outs[chunk * seq_count + shift]
            head = lax.rem(lax.axis_index("seq") + shift, seq_count) * per_place + chunk
            for n in range(3):
                out[n * rows : (n + 1) * rows, :] = wide[
                    n, pl.ds(head, rows, stride=heads), :
                ].astype(jnp.bfloat16)
            out[3 * rows :, :] = meta.astype(jnp.bfloat16)
    copies[-1].wait()


def half_sums(array, ones_block):
    high = array.astype(jnp.bfloat16)
    low = (array - high.astype(jnp.float32)).astype(jnp.bfloat16)
    return dot_nn(high, ones_block) + dot_nn(low, ones_block)


def signed_features(inputs, weights, ones_block, left):
    first = weights.astype(jnp.bfloat16)
    left_over = weights - first.astype(jnp.float32)
    second = left_over.astype(jnp.bfloat16)
    third = (left_over - second.astype(jnp.float32)).astype(jnp.bfloat16)
    logits = dot_nn(inputs, first) + dot_nn(inputs, second) + dot_nn(inputs, third)
    left_most = jnp.max(jnp.where(left, logits, -jnp.inf), axis=1, keepdims=True)
    right_most = jnp.max(jnp.where(left, -jnp.inf, logits), axis=1, keepdims=True)
    raised = jnp.exp2((logits - jnp.where(left, left_most, right_most)) * LOG2E)
    return raised / half_sums(raised, ones_block)


def ones_halves():
    row = lax.broadcasted_iota(jnp.int32, (LANES, LANES), 0) < LANES // 2
    col = lax.broadcasted_iota(jnp.int32, (LANES, LANES), 1) < LANES // 2
    return (row == col).astype(jnp.bfloat16)


def block_places(first, bounds):
    place = lax.broadcasted_iota(jnp.int32, (BLOCK, LANES), 0) + first
    start = jnp.zeros((BLOCK, LANES), jnp.int32)
    for value in range(DOC_VALUES - 1):
        bound = bounds[value : value + 1, :]
        start = jnp.maximum(start, jnp.where(bound <= place, bound, 0))
    return place[:, :1], start[:, :1]


def forward_kernel(seq_count, chunk, score_scale, normaliser, *refs):
    pieces, map_ref, earlier_ref = refs[:seq_count], refs[seq_count], refs[seq_count + 1]
    outs = refs[seq_count + 2 : 2 * seq_count + 2]
    loss_ref, qkv_ref, feat_ref, slope_ref, bound_ref = refs[
        2 * seq_count + 2 : 2 * seq_count + 7
    ]
    v_s, t_s, s_s, qb_s, kb_s = refs[2 * seq_count + 7 :]
    q_s, k_s = qkv_ref.at[0], qkv_ref.at[1]
    total = v_s.shape[0]
    rows = total // seq_count
    exponent = score_scale * LOG2E

    counts = jnp.zeros((META_ROWS, LANES), jnp.float32)
    for shift, piece in enumerate(pieces):
        span = pl.ds(pl.multiple_of(place_of(shift, seq_count) * rows, 16), rows)
        for n in range(3):
            qkv_ref[n, span, :] = piece[n * rows : (n + 1) * rows, :]
        v_s[span, :LANES] = piece[2 * rows : 3 * rows, :]
        counts = counts + piece[3 * rows :, :].astype(jnp.float32)
    v_s[:, LANES:] = jnp.ones((total, LANES), jnp.bfloat16)
    bounds = counts.astype(jnp.int32)
    bound_ref[...] = bounds

    lane = lax.broadcasted_iota(jnp.int32, (1, LANES), 1)
    left = lane < LANES // 2
    ones_block = ones_halves()
    weights = map_ref[chunk]
    rolled = pltpu.roll(weights, LANES // 2, 1)
    q_feat = signed_features(q_s[...], jnp.where(left, weights, -rolled), ones_block, left)
    k_feat = signed_features(k_s[...], jnp.where(left, rolled, -weights), ones_block, left)
    feat_ref[0] = q_feat
    feat_ref[1] = k_feat
    qb_s[...] = q_feat.astype(jnp.bfloat16)
    kb_s[...] = k_feat.astype(jnp.bfloat16)
    loss = jnp.zeros((8, LANES), jnp.float32)

    for first in range(0, total, BLOCK):
        last = first + BLOCK
        near = max(0, first - LANES)
        row, start = block_places(first, bounds)
        col = lax.broadcasted_iota(jnp.int32, (BLOCK, last), 1)
        visible = (col <= row) & (col >= start)
        far = (col <= row - WINDOW) & (col >= start)
        window = visible[:, near:] & (col[:, near:] > row - WINDOW)
        scores = dot_nt(q_s[first:last, :], k_s[:last, :])
        shown = jnp.where(visible, scores, masked_value)
        raised = jnp.exp2((shown - jnp.max(shown, axis=1, keepdims=True)) * exponent)
        numer = dot_nn(raised.astype(jnp.bfloat16), v_s[:last, :LANES])
        teacher = (numer / jnp.sum(raised, axis=1, keepdims=True)).astype(jnp.bfloat16)
        t_s[first:last, :] = teacher

        shown = jnp.where(window, scores[:, near:], masked_value)
        raised = jnp.exp2((shown - jnp.max(shown, axis=1, keepdims=True)) * exponent)
        linear = dot_nt(qb_s[first:last, :], kb_s[:last, :])
        weight = jnp.where(far[:, near:], linear[:, near:], raised)
        if near:
            weight = jnp.concatenate(
                [jnp.where(far[:, :near], linear[:, :near], 0.0), weight], axis=1
            )
        sums = dot_nn(weight.astype(jnp.bfloat16), v_s[:last, :])
        inverse = 1.0 / sums[:, LANES:]
        output = sums[:, :LANES] * inverse
        s_s[first:last, :] = output.astype(jnp.bfloat16)
        error = output - teacher.astype(jnp.float32)
        loss = loss + jnp.sum((error * error).reshape(BLOCK // 8, 8, LANES), axis=0)

        slope = error * (2.0 * normaliser)
        slope_denom = -jnp.sum(slope * output, axis=1, keepdims=True) * inverse
        high = slope_denom.astype(jnp.bfloat16).astype(jnp.float32)
        extra = jnp.where(lane == 0, high, jnp.where(lane == 1, slope_denom - high, 0.0))
        slope_ref[first:last, :LANES] = (slope * inverse).astype(jnp.bfloat16)
        slope_ref[first:last, LANES:] = extra.astype(jnp.bfloat16)

    for shift, out in enumerate(outs):
        first = lax.rem(lax.axis_index("seq") + shift, seq_count) * rows
        span = pl.ds(pl.multiple_of(first, 16), rows)
        out[:rows, :] = t_s[span, :]
        out[rows:, :] = s_s[span, :]
    loss_ref[...] = earlier_ref[...] + jnp.sum(loss) * normaliser


def backward_kernel(per_place, *refs):
    saved, grad_ref = refs[: 4 * per_place], refs[4 * per_place]
    v_s, qb_s, kb_s, dq_s, dk_s = refs[4 * per_place + 1 :]
    total = v_s.shape[0]
    left = lax.broadcasted_iota(jnp.int32, (1, LANES), 1) < LANES // 2
    ones_block = ones_halves()

    def logits_slope(feat, slope):
        product = feat * slope
        return (product - feat * half_sums(product, ones_block)).astype(jnp.bfloat16)

    for chunk in range(per_place):
        qkv_ref, feat_ref, slope_ref, bound_ref = saved[4 * chunk : 4 * chunk + 4]
        bounds = bound_ref[...]
        v_s[:, :LANES] = qkv_ref[2]
        v_s[:, LANES:] = jnp.ones((total, LANES), jnp.bfloat16)
        qb_s[...] = feat_ref[0].astype(jnp.bfloat16)
        kb_s[...] = feat_ref[1].astype(jnp.bfloat16)
        dk_s[...] = jnp.zeros_like(dk_s)
        for first in range(0, total, BLOCK):
            last = first + BLOCK
            row, start = block_places(first, bounds)
            col = lax.broadcasted_iota(jnp.int32, (BLOCK, last), 1)
            far = (col <= row - WINDOW) & (col >= start)
            slope_weight = jnp.where(
                far, dot_nt(slope_ref[first:last, :], v_s[:last, :]), 0.0
            ).astype(jnp.bfloat16)
            dq_s[first:last, :] = dot_nn(slope_weight, kb_s[:last, :])
            dk_s[:last, :] += dot_tn(slope_weight, qb_s[first:last, :])
        from_q = dot_tn(qkv_ref[0], logits_slope(feat_ref[0], dq_s[...]))
        from_k = dot_tn(qkv_ref[1], logits_slope(feat_ref[1], dk_s[...]))
        grad_ref[chunk * LANES : (chunk + 1) * LANES, :] = jnp.where(
            left,
            from_q - pltpu.roll(from_q, LANES // 2, 1),
            pltpu.roll(from_k, LANES // 2, 1) - from_k,
        ).astype(jnp.bfloat16)


def unpack_kernel(seq_count, per_place, *refs):
    pieces = refs[: seq_count * per_place]
    t_ref, s_ref, t_wide, s_wide = refs[seq_count * per_place :]
    heads = seq_count * per_place
    rows = t_ref.shape[0] // heads
    for chunk in range(per_place):
        for shift in range(seq_count):
            piece = pieces[chunk * seq_count + shift]
            head = place_of(shift, seq_count) * per_place + chunk
            t_wide[pl.ds(head, rows, stride=heads), :] = piece[:rows, :].astype(jnp.float32)
            s_wide[pl.ds(head, rows, stride=heads), :] = piece[rows : 2 * rows, :].astype(
                jnp.float32
            )
    t_ref[...] = t_wide[...].astype(jnp.bfloat16)
    s_ref[...] = s_wide[...].astype(jnp.bfloat16)


def join_kernel(grad_ref, *refs):
    losses, out = refs[:-1], refs[-1]
    size = grad_ref.shape[0]
    loss = losses[0][...]
    if len(losses) == 4:
        loss = (loss + losses[2][...]) + (losses[1][...] + losses[3][...])
    out[:size, :] = grad_ref[...]
    row = lax.broadcasted_iota(jnp.int32, (8, LANES), 0)
    high = loss.astype(jnp.bfloat16).astype(jnp.float32)
    middle = (loss - high).astype(jnp.bfloat16).astype(jnp.float32)
    low = (loss - high) - middle
    parts = jnp.where(row == 0, high, jnp.where(row == 1, middle, jnp.where(row == 2, low, 0.0)))
    out[size:, :] = jnp.concatenate([parts, parts], axis=0).astype(jnp.bfloat16)


def final_kernel(seq_count, per_place, *refs):
    pieces = refs[:seq_count]
    grad_ref, loss_ref, parts_s = refs[seq_count:]
    for shift, piece in enumerate(pieces):
        source = place_of(shift, seq_count)
        for chunk in range(per_place):
            grad_ref[source * per_place + chunk] = piece[
                chunk * LANES : (chunk + 1) * LANES, :
            ].astype(jnp.float32)
        tail = piece[per_place * LANES :, :].astype(jnp.float32)
        parts_s[source] = tail[0:1, :] + tail[1:2, :] + tail[2:3, :]
    loss = parts_s[0]
    for source in range(1, seq_count):
        loss = loss + parts_s[source]
    loss_ref[...] = loss


def kernel_call(
    kernel, out_shape, scratch_shapes, flops, moved, name, vmem=48, **specs
):
    return pl.pallas_call(
        kernel,
        **specs,
        out_shape=out_shape,
        scratch_shapes=scratch_shapes,
        compiler_params=pltpu.CompilerParams(vmem_limit_bytes=vmem * 1024 * 1024),
        cost_estimate=pl.CostEstimate(flops=flops, bytes_accessed=moved, transcendentals=0),
        name=name,
    )


def split_body(queries, keys, values, documents, feature_map):
    tok_rows, head_count, head_width = queries.shape
    seq_count = lax.axis_size("seq")
    per_place = head_count // seq_count
    total = tok_rows * seq_count
    score_scale = head_width ** (-0.5)
    normaliser = 1.0 / (total * head_count * lax.axis_size(("grp", "head")))
    flat = [a.reshape(tok_rows * head_count, head_width) for a in (queries, keys, values)]
    docs = documents.reshape(1, tok_rows)
    sent_rows = 3 * tok_rows + META_ROWS
    bf16, f32 = jnp.bfloat16, jnp.float32

    def sizes(*rows, dtype=bf16):
        return [jax.ShapeDtypeStruct((n, LANES), dtype) for n in rows]

    def sent(blocks):
        return [blocks[0]] + [turned(blocks[d], "seq", d) for d in range(1, seq_count)]

    def after(blocks, arrived):
        blocks, passed = lax.optimization_barrier((blocks, arrived[1:]))
        return blocks, arrived[:1] + passed

    *packed, own_map = kernel_call(
        functools.partial(pack_kernel, seq_count, per_place),
        sizes(*[sent_rows] * head_count)
        + [jax.ShapeDtypeStruct((per_place,) + feature_map.shape[1:], f32)],
        [
            pltpu.VMEM((3, tok_rows * head_count, LANES), bf16),
            pltpu.VMEM((3, tok_rows * head_count, LANES), f32),
            pltpu.SemaphoreType.DMA((3 * COPIES + 1,)),
        ],
        0,
        12 * tok_rows * head_count * LANES,
        "pack",
        vmem=PACK_VMEM,
        in_specs=[pl.BlockSpec(memory_space=pltpu.HBM)] * 4
        + [pl.BlockSpec(memory_space=pltpu.VMEM)],
    )(*flat, feature_map, docs)
    held = [
        sent(packed[chunk * seq_count : (chunk + 1) * seq_count]) for chunk in range(per_place)
    ]

    returned, saved = [], []
    loss = jnp.zeros((8, LANES), f32)
    for chunk in range(per_place):
        results = kernel_call(
            functools.partial(forward_kernel, seq_count, chunk, score_scale, normaliser),
            sizes(*[2 * tok_rows] * seq_count)
            + sizes(8, dtype=f32)
            + [
                jax.ShapeDtypeStruct((3, total, LANES), bf16),
                jax.ShapeDtypeStruct((2, total, LANES), f32),
                jax.ShapeDtypeStruct((total, 2 * LANES), bf16),
                jax.ShapeDtypeStruct((META_ROWS, LANES), jnp.int32),
            ],
            [
                pltpu.VMEM((total, 2 * LANES), bf16),
                pltpu.VMEM((total, LANES), bf16),
                pltpu.VMEM((total, LANES), bf16),
                pltpu.VMEM((total, LANES), bf16),
                pltpu.VMEM((total, LANES), bf16),
            ],
            HEAD_COST,
            16 * total * LANES,
            "forward",
        )(*held[chunk], own_map, loss)
        loss = results[seq_count]
        saved.append(results[seq_count + 1 :])
        returned.append(sent(results[:seq_count]))

    saved, returned[0] = after(saved, returned[0])
    grad = kernel_call(
        functools.partial(backward_kernel, per_place),
        sizes(per_place * LANES)[0],
        [
            pltpu.VMEM((total, 2 * LANES), bf16),
            pltpu.VMEM((total, LANES), bf16),
            pltpu.VMEM((total, LANES), bf16),
            pltpu.VMEM((total, LANES), f32),
            pltpu.VMEM((total, LANES), f32),
        ],
        HEAD_COST,
        16 * total * LANES,
        "backward",
    )(*[part for parts in saved for part in parts])
    loss = summed_over(loss, "grp")
    if lax.axis_size("head") == 4:
        losses = [loss] + [crossed(loss, "head", mask) for mask in range(1, 4)]
    else:
        losses = [summed_over(loss, "head")]
    for n in range(1, per_place):
        grad, returned[n] = after(grad, returned[n])
    joined = kernel_call(
        join_kernel,
        sizes(per_place * LANES + META_ROWS)[0],
        [],
        0,
        16 * LANES * LANES,
        "join",
    )(grad, *losses)
    last = sent([joined] * seq_count)
    teacher_out, student_out = kernel_call(
        functools.partial(unpack_kernel, seq_count, per_place),
        sizes(*[tok_rows * head_count] * 2),
        [pltpu.VMEM((tok_rows * head_count, LANES), f32)] * 2,
        0,
        12 * tok_rows * head_count * LANES,
        "unpack",
    )(*[piece for pieces in returned for piece in pieces])
    feature_grad, loss = kernel_call(
        functools.partial(final_kernel, seq_count, per_place),
        [jax.ShapeDtypeStruct(feature_map.shape, f32)] + sizes(1, dtype=f32),
        [pltpu.VMEM((seq_count, 1, LANES), f32)],
        0,
        8 * head_count * LANES * LANES,
        "final",
    )(*last)
    return (
        teacher_out.reshape(queries.shape),
        student_out.reshape(queries.shape),
        loss[0, 0],
        feature_grad,
    )


def body(queries, keys, values, documents, feature_map):
    tok_rows, head_count, head_width = queries.shape
    if fits_split(tok_rows, head_count, head_width, feature_map.shape[2], lax.axis_size("seq")):
        return split_body(queries, keys, values, documents, feature_map)
    return relay_body(queries, keys, values, documents, feature_map)


def solution(mesh):
    in_specs = (
        P("seq", ("grp", "head"), None),
        P("seq", ("grp", "head"), None),
        P("seq", ("grp", "head"), None),
        P("seq"),
        P(("grp", "head"), None, None),
    )
    out_specs = (
        P("seq", ("grp", "head"), None),
        P("seq", ("grp", "head"), None),
        P(),
        P(("grp", "head"), None, None),
    )
    return jax.shard_map(body, mesh=mesh, in_specs=in_specs, out_specs=out_specs, check_vma=False)
```

```python
import functools
import math

import jax
import jax.numpy as jnp
from jax import lax
from jax.experimental import pallas as pl
from jax.experimental.pallas import tpu as pltpu
from jax.sharding import PartitionSpec as P

WINDOW = 64
DOC_VALUES = 4
LANES = 128
META_ROWS = 16
BLOCK = 256
LOG2E = math.log2(math.e)
COPIES = 4

PACK_VMEM = 60
HEAD_COST = 6_000_000_000


exact_mode = lax.Precision.HIGHEST
masked_value = -1e30


def passed_along(block, axis, distance):
    devices = range(lax.axis_size(axis))
    route = [(i - distance, i) for i in devices if i - distance in devices]
    return lax.ppermute(block, axis, route)


def features(inputs, weights):
    logits = jnp.einsum("rhd,hdf->rhf", inputs, weights, precision=exact_mode)
    return jnp.concatenate(
        [jax.nn.softmax(logits, axis=-1), jax.nn.softmax(-logits, axis=-1)], axis=-1
    )


def join_up(earlier, later):
    merged_tag = jnp.maximum(earlier[0], later[0])
    early_keep = (earlier[0] == merged_tag).astype(earlier[1].dtype)
    late_keep = (later[0] == merged_tag).astype(later[1].dtype)
    return (
        merged_tag,
        early_keep * earlier[1] + late_keep * later[1],
        early_keep * earlier[2] + late_keep * later[2],
    )


def join_down(earlier, later):
    merged_tag = jnp.minimum(earlier[0], later[0])
    early_keep = (earlier[0] == merged_tag).astype(earlier[1].dtype)
    late_keep = (later[0] == merged_tag).astype(later[1].dtype)
    return (
        merged_tag,
        early_keep * earlier[1] + late_keep * later[1],
        early_keep * earlier[2] + late_keep * later[2],
    )


def relay_body(queries, keys, values, documents, feature_map):
    tok_rows, head_count, head_width = queries.shape
    half_feat = feature_map.shape[2] // 2
    score_scale = head_width ** (-0.5)
    seq_place = lax.axis_index("seq")
    seq_count = lax.axis_size("seq")
    first_row = seq_place * tok_rows
    doc_float = documents.astype(jnp.float32)
    doc_marks = (documents + 1).astype(jnp.bfloat16)
    query_pos = first_row + jnp.arange(tok_rows)

    def attend(carried, portion):
        key_piece, value_piece, mark_piece = portion
        key_pos = jnp.arange(key_piece.shape[0])
        same_doc = mark_piece.astype(jnp.float32)[None, :] - 1.0 == doc_float[:, None]
        allowed = (same_doc & (key_pos[None, :] <= query_pos[:, None]))[:, None, :]
        scores = (
            jnp.einsum("ihd,jhd->ihj", queries, key_piece, preferred_element_type=jnp.float32)
            * score_scale
        )
        scores = jnp.where(allowed, scores, masked_value)
        row_max, totals, numerator = carried
        new_max = jnp.maximum(row_max, jnp.max(scores, axis=-1))
        probabilities = jnp.where(allowed, jnp.exp(scores - new_max[:, :, None]), 0.0)
        totals = jnp.sum(probabilities, axis=-1)
        numerator = jnp.einsum(
            "ihj,jhd->ihd",
            probabilities.astype(jnp.bfloat16),
            value_piece,
            preferred_element_type=jnp.float32,
        )
        return (new_max, totals, numerator)

    start_carry = (
        jnp.full((tok_rows, head_count), masked_value, jnp.float32),
        jnp.zeros((tok_rows, head_count), jnp.float32),
        jnp.zeros((tok_rows, head_count, head_width), jnp.float32),
    )
    portion = (
        lax.all_gather(keys, "seq", axis=0, tiled=True),
        lax.all_gather(values, "seq", axis=0, tiled=True),
        lax.all_gather(doc_marks, "seq", axis=0, tiled=True),
    )
    touches = (jnp.int32(0) < first_row + tok_rows) & (
        portion[2][-1].astype(jnp.float32) - 1.0 >= doc_float[0]
    )

    def compute_update(held_carry):
        return attend(held_carry, portion)

    def keep_carry(held_carry):
        return held_carry

    row_max, totals, numerator = lax.cond(touches, compute_update, keep_carry, start_carry)
    teacher_out = (numerator / totals[:, :, None]).astype(jnp.bfloat16)
    target = teacher_out.astype(jnp.float32)
    halo_keys, halo_values, halo_marks = passed_along(
        (keys[tok_rows - WINDOW :], values[tok_rows - WINDOW :], doc_marks[tok_rows - WINDOW :]),
        "seq",
        1,
    )
    key_joined = jnp.concatenate([halo_keys, keys], axis=0)
    key_float = key_joined.astype(jnp.float32)
    value_float = jnp.concatenate([halo_values, values], axis=0).astype(jnp.float32)
    doc_all = jnp.concatenate([halo_marks.astype(jnp.float32) - 1.0, doc_float], axis=0)
    query_float = queries.astype(jnp.float32)
    distance = jnp.arange(tok_rows)[:, None] + WINDOW - jnp.arange(tok_rows + WINDOW)[None, :]
    same_doc = doc_float[:, None] == doc_all[None, :]
    in_window = same_doc & (distance >= 0) & (distance < WINDOW)
    beyond = same_doc & (distance >= WINDOW)
    scores = (
        jnp.einsum("ihd,jhd->hij", queries, key_joined, preferred_element_type=jnp.float32)
        * score_scale
    )
    window_row = jnp.max(jnp.where(in_window[None], scores, masked_value), axis=-1, keepdims=True)
    window_weight = jnp.where(in_window[None], jnp.exp(scores - window_row), 0.0)
    elem_keys = key_float[:tok_rows]
    elem_values = value_float[:tok_rows]
    elem_docs = doc_all[:tok_rows]
    elem_tag = elem_docs[tok_rows - 1]
    in_tail = (elem_docs == elem_tag).astype(jnp.float32)

    def element(weights):
        masked_feat = features(elem_keys, weights[:, :, half_feat:]) * in_tail[:, None, None]
        return (
            jnp.einsum("jhf,jhd->hfd", masked_feat, elem_values, precision=exact_mode),
            jnp.sum(masked_feat, axis=0),
        )

    (elem_state, elem_norm), element_pullback = jax.vjp(element, feature_map)
    blank_state = jnp.zeros_like(elem_state)
    blank_norm = jnp.zeros_like(elem_norm)
    forward_blank = (jnp.float32(-2.0), blank_state, blank_norm)

    def relay_step(turn_index, carried):
        arrived = passed_along(join_up(carried, (elem_tag, elem_state, elem_norm)), "seq", 1)
        return jax.tree.map(
            lambda received, blank_entry: jnp.where(seq_place == 0, blank_entry, received),
            arrived,
            forward_blank,
        )

    tag_in, state_in, norm_in = lax.fori_loop(0, seq_count - 1, relay_step, forward_blank)
    uses_state = (doc_float == tag_in).astype(jnp.float32)[:, None]
    normaliser = 1.0 / (tok_rows * seq_count * head_count * lax.axis_size(("grp", "head")))

    def local_loss(weights, state, norm):
        query_feat = features(query_float, weights[:, :, :half_feat])
        key_feat = features(key_float, weights[:, :, half_feat:])
        linear = jnp.where(
            beyond[None],
            jnp.einsum("ihf,jhf->hij", query_feat, key_feat, precision=exact_mode),
            0.0,
        )
        weight = window_weight + linear
        numer_sum = jnp.einsum("hij,jhd->ihd", weight, value_float, precision=exact_mode)
        numer_sum = numer_sum + uses_state[:, :, None] * jnp.einsum(
            "ihf,hfd->ihd", query_feat, state, precision=exact_mode
        )
        denominator = jnp.sum(weight, axis=-1).T + uses_state * jnp.einsum(
            "ihf,hf->ih", query_feat, norm, precision=exact_mode
        )
        output = numer_sum / denominator[:, :, None]
        return (jnp.sum(jnp.square(output - target)) * normaliser, output)

    local_part, local_pullback, output = jax.vjp(
        local_loss, feature_map, state_in, norm_in, has_aux=True
    )
    grad_direct, grad_state, grad_norm = local_pullback(jnp.ones_like(local_part))
    backward_blank = (jnp.float32(1000000000.0), blank_state, blank_norm)

    def return_step(turn_index, carried):
        arrived = passed_along(join_down(carried, (tag_in, grad_state, grad_norm)), "seq", -1)
        return jax.tree.map(
            lambda received, blank_entry: jnp.where(
                seq_place == seq_count - 1, blank_entry, received
            ),
            arrived,
            backward_blank,
        )

    back_tag, carried_state, carried_norm = lax.fori_loop(
        0, seq_count - 1, return_step, backward_blank
    )
    total_grad = grad_direct + element_pullback((carried_state, carried_norm))[0]
    feature_grad = lax.psum(total_grad, "seq")
    loss_total = lax.psum(local_part, ("grp", "seq", "head"))
    return (teacher_out, output.astype(jnp.bfloat16), loss_total, feature_grad)


def turned(block, axis, distance):
    count = lax.axis_size(axis)
    return lax.ppermute(block, axis, [(i, (i + distance) % count) for i in range(count)])


def crossed(block, axis, mask):
    count = lax.axis_size(axis)
    return lax.ppermute(block, axis, [(i, i ^ mask) for i in range(count)])


def summed_over(block, axis):
    count = lax.axis_size(axis)
    if count == 1:
        return block
    if count == 2:
        return block + crossed(block, axis, 1)
    if count == 4:
        return (block + crossed(block, axis, 2)) + (
            crossed(block, axis, 1) + crossed(block, axis, 3)
        )
    return lax.psum(block, axis)


def fits_split(tok_rows, head_count, head_width, feat, seq_count):
    return (
        head_count % seq_count == 0
        and head_count % 8 == 0
        and tok_rows % 16 == 0
        and tok_rows <= 256
        and tok_rows * seq_count <= 1536
        and (tok_rows * seq_count) % BLOCK == 0
        and head_width == LANES
        and feat == LANES
    )


def dot_nn(a, b):
    return jnp.dot(a, b, preferred_element_type=jnp.float32)


def dot_nt(a, b):
    return lax.dot_general(a, b, (((1,), (1,)), ((), ())), preferred_element_type=jnp.float32)


def dot_tn(a, b):
    return lax.dot_general(a, b, (((0,), (0,)), ((), ())), preferred_element_type=jnp.float32)


def place_of(shift, seq_count):
    return lax.rem(lax.axis_index("seq") + (seq_count - shift), seq_count)


def deal(wide, docs, parts, outs, seq_count, per_place):
    rows = docs.shape[1]
    heads = seq_count * per_place
    meta_row = lax.broadcasted_iota(jnp.int32, (META_ROWS, LANES), 0)
    meta = jnp.zeros((META_ROWS, LANES), jnp.float32)
    for value in range(DOC_VALUES - 1):
        amount = jnp.sum((docs <= value).astype(jnp.float32), axis=1, keepdims=True)
        meta = jnp.where(meta_row == value, amount, meta)
    for (chunk, shift), out in zip(parts, outs):
        head = lax.rem(lax.axis_index("seq") + shift, seq_count) * per_place + chunk
        for n in range(3):
            out[n * rows : (n + 1) * rows, :] = wide[
                n, pl.ds(head, rows, stride=heads), :
            ].astype(jnp.bfloat16)
        out[3 * rows :, :] = meta.astype(jnp.bfloat16)


def pack_kernel(seq_count, per_place, parts, q_ref, k_ref, v_ref, doc_ref, *rest):
    outs, (narrow, wide, docs, sems) = rest[: len(parts)], rest[len(parts) :]
    part = narrow.shape[1] // COPIES
    copies = []
    for n, ref in enumerate((q_ref, k_ref, v_ref)):
        for piece in range(COPIES):
            span = pl.ds(piece * part, part)
            copies.append(
                pltpu.make_async_copy(
                    ref.at[span, :], narrow.at[n, span, :], sems.at[n * COPIES + piece]
                )
            )
    copies.append(pltpu.make_async_copy(doc_ref, docs, sems.at[3 * COPIES]))
    for copy in copies:
        copy.start()
    for n in range(3):
        for piece in range(COPIES):
            copies[n * COPIES + piece].wait()
            span = pl.ds(piece * part, part)
            wide[n, span, :] = narrow[n, span, :].astype(jnp.float32)
    copies[-1].wait()
    deal(wide, docs[...], parts, outs, seq_count, per_place)


def pack_rest_kernel(seq_count, per_place, parts, q_ref, k_ref, v_ref, doc_ref, map_ref, *rest):
    outs, (own_map, wide) = rest[: len(parts)], rest[len(parts) :]
    for n, ref in enumerate((q_ref, k_ref, v_ref)):
        wide[n] = ref[...].astype(jnp.float32)
    deal(wide, doc_ref[...], parts, outs, seq_count, per_place)
    for chunk in range(per_place):
        own_map[chunk] = map_ref[lax.axis_index("seq") * per_place + chunk]


def half_sums(array, ones_block):
    high = array.astype(jnp.bfloat16)
    low = (array - high.astype(jnp.float32)).astype(jnp.bfloat16)
    return dot_nn(high, ones_block) + dot_nn(low, ones_block)


def signed_features(inputs, weights, ones_block, left):
    first = weights.astype(jnp.bfloat16)
    left_over = weights - first.astype(jnp.float32)
    second = left_over.astype(jnp.bfloat16)
    third = (left_over - second.astype(jnp.float32)).astype(jnp.bfloat16)
    logits = dot_nn(inputs, first) + dot_nn(inputs, second) + dot_nn(inputs, third)
    left_most = jnp.max(jnp.where(left, logits, -jnp.inf), axis=1, keepdims=True)
    right_most = jnp.max(jnp.where(left, -jnp.inf, logits), axis=1, keepdims=True)
    raised = jnp.exp2((logits - jnp.where(left, left_most, right_most)) * LOG2E)
    return raised / half_sums(raised, ones_block)


def ones_halves():
    row = lax.broadcasted_iota(jnp.int32, (LANES, LANES), 0) < LANES // 2
    col = lax.broadcasted_iota(jnp.int32, (LANES, LANES), 1) < LANES // 2
    return (row == col).astype(jnp.bfloat16)


def block_places(first, bounds):
    place = lax.broadcasted_iota(jnp.int32, (BLOCK, LANES), 0) + first
    start = jnp.zeros((BLOCK, LANES), jnp.int32)
    for value in range(DOC_VALUES - 1):
        bound = bounds[value : value + 1, :]
        start = jnp.maximum(start, jnp.where(bound <= place, bound, 0))
    return place[:, :1], start[:, :1]


def forward_kernel(seq_count, chunk, score_scale, normaliser, *refs):
    pieces, map_ref, earlier_ref = refs[:seq_count], refs[seq_count], refs[seq_count + 1]
    outs = refs[seq_count + 2 : 2 * seq_count + 2]
    loss_ref, qkv_ref, feat_ref, slope_ref, bound_ref = refs[
        2 * seq_count + 2 : 2 * seq_count + 7
    ]
    v_s, t_s, s_s, qb_s, kb_s = refs[2 * seq_count + 7 :]
    q_s, k_s = qkv_ref.at[0], qkv_ref.at[1]
    total = v_s.shape[0]
    rows = total // seq_count
    exponent = score_scale * LOG2E

    counts = jnp.zeros((META_ROWS, LANES), jnp.float32)
    for shift, piece in enumerate(pieces):
        span = pl.ds(pl.multiple_of(place_of(shift, seq_count) * rows, 16), rows)
        for n in range(3):
            qkv_ref[n, span, :] = piece[n * rows : (n + 1) * rows, :]
        v_s[span, :LANES] = piece[2 * rows : 3 * rows, :]
        counts = counts + piece[3 * rows :, :].astype(jnp.float32)
    v_s[:, LANES:] = jnp.ones((total, LANES), jnp.bfloat16)
    bounds = counts.astype(jnp.int32)
    bound_ref[...] = bounds

    lane = lax.broadcasted_iota(jnp.int32, (1, LANES), 1)
    left = lane < LANES // 2
    ones_block = ones_halves()
    weights = map_ref[chunk]
    rolled = pltpu.roll(weights, LANES // 2, 1)
    q_feat = signed_features(q_s[...], jnp.where(left, weights, -rolled), ones_block, left)
    k_feat = signed_features(k_s[...], jnp.where(left, rolled, -weights), ones_block, left)
    feat_ref[0] = q_feat
    feat_ref[1] = k_feat
    qb_s[...] = q_feat.astype(jnp.bfloat16)
    kb_s[...] = k_feat.astype(jnp.bfloat16)
    loss = jnp.zeros((8, LANES), jnp.float32)

    for first in range(0, total, BLOCK):
        last = first + BLOCK
        near = max(0, first - LANES)
        row, start = block_places(first, bounds)
        col = lax.broadcasted_iota(jnp.int32, (BLOCK, last), 1)
        visible = (col <= row) & (col >= start)
        far = (col <= row - WINDOW) & (col >= start)
        window = visible[:, near:] & (col[:, near:] > row - WINDOW)
        scores = dot_nt(q_s[first:last, :], k_s[:last, :])
        shown = jnp.where(visible, scores, masked_value)
        raised = jnp.exp2((shown - jnp.max(shown, axis=1, keepdims=True)) * exponent)
        numer = dot_nn(raised.astype(jnp.bfloat16), v_s[:last, :LANES])
        teacher = (numer / jnp.sum(raised, axis=1, keepdims=True)).astype(jnp.bfloat16)
        t_s[first:last, :] = teacher

        shown = jnp.where(window, scores[:, near:], masked_value)
        raised = jnp.exp2((shown - jnp.max(shown, axis=1, keepdims=True)) * exponent)
        linear = dot_nt(qb_s[first:last, :], kb_s[:last, :])
        weight = jnp.where(far[:, near:], linear[:, near:], raised)
        if near:
            weight = jnp.concatenate(
                [jnp.where(far[:, :near], linear[:, :near], 0.0), weight], axis=1
            )
        sums = dot_nn(weight.astype(jnp.bfloat16), v_s[:last, :])
        inverse = 1.0 / sums[:, LANES:]
        output = sums[:, :LANES] * inverse
        s_s[first:last, :] = output.astype(jnp.bfloat16)
        error = output - teacher.astype(jnp.float32)
        loss = loss + jnp.sum((error * error).reshape(BLOCK // 8, 8, LANES), axis=0)

        slope = error * (2.0 * normaliser)
        slope_denom = -jnp.sum(slope * output, axis=1, keepdims=True) * inverse
        high = slope_denom.astype(jnp.bfloat16).astype(jnp.float32)
        extra = jnp.where(lane == 0, high, jnp.where(lane == 1, slope_denom - high, 0.0))
        slope_ref[first:last, :LANES] = (slope * inverse).astype(jnp.bfloat16)
        slope_ref[first:last, LANES:] = extra.astype(jnp.bfloat16)

    for shift, out in enumerate(outs):
        first = lax.rem(lax.axis_index("seq") + shift, seq_count) * rows
        span = pl.ds(pl.multiple_of(first, 16), rows)
        out[:rows, :] = t_s[span, :]
        out[rows:, :] = s_s[span, :]
    loss_ref[...] = earlier_ref[...] + jnp.sum(loss) * normaliser


def backward_kernel(per_place, *refs):
    saved, grad_ref = refs[: 4 * per_place], refs[4 * per_place]
    v_s, qb_s, kb_s, dq_s, dk_s = refs[4 * per_place + 1 :]
    total = v_s.shape[0]
    left = lax.broadcasted_iota(jnp.int32, (1, LANES), 1) < LANES // 2
    ones_block = ones_halves()

    def logits_slope(feat, slope):
        product = feat * slope
        return (product - feat * half_sums(product, ones_block)).astype(jnp.bfloat16)

    for chunk in range(per_place):
        qkv_ref, feat_ref, slope_ref, bound_ref = saved[4 * chunk : 4 * chunk + 4]
        bounds = bound_ref[...]
        v_s[:, :LANES] = qkv_ref[2]
        v_s[:, LANES:] = jnp.ones((total, LANES), jnp.bfloat16)
        qb_s[...] = feat_ref[0].astype(jnp.bfloat16)
        kb_s[...] = feat_ref[1].astype(jnp.bfloat16)
        dk_s[...] = jnp.zeros_like(dk_s)
        for first in range(0, total, BLOCK):
            last = first + BLOCK
            row, start = block_places(first, bounds)
            col = lax.broadcasted_iota(jnp.int32, (BLOCK, last), 1)
            far = (col <= row - WINDOW) & (col >= start)
            slope_weight = jnp.where(
                far, dot_nt(slope_ref[first:last, :], v_s[:last, :]), 0.0
            ).astype(jnp.bfloat16)
            dq_s[first:last, :] = dot_nn(slope_weight, kb_s[:last, :])
            dk_s[:last, :] += dot_tn(slope_weight, qb_s[first:last, :])
        from_q = dot_tn(qkv_ref[0], logits_slope(feat_ref[0], dq_s[...]))
        from_k = dot_tn(qkv_ref[1], logits_slope(feat_ref[1], dk_s[...]))
        grad_ref[chunk * LANES : (chunk + 1) * LANES, :] = jnp.where(
            left,
            from_q - pltpu.roll(from_q, LANES // 2, 1),
            pltpu.roll(from_k, LANES // 2, 1) - from_k,
        ).astype(jnp.bfloat16)


def unpack_kernel(seq_count, per_place, *refs):
    pieces = refs[: seq_count * per_place]
    t_ref, s_ref, t_wide, s_wide = refs[seq_count * per_place :]
    heads = seq_count * per_place
    rows = t_ref.shape[0] // heads
    for chunk in range(per_place):
        for shift in range(seq_count):
            piece = pieces[chunk * seq_count + shift]
            head = place_of(shift, seq_count) * per_place + chunk
            t_wide[pl.ds(head, rows, stride=heads), :] = piece[:rows, :].astype(jnp.float32)
            s_wide[pl.ds(head, rows, stride=heads), :] = piece[rows : 2 * rows, :].astype(
                jnp.float32
            )
    t_ref[...] = t_wide[...].astype(jnp.bfloat16)
    s_ref[...] = s_wide[...].astype(jnp.bfloat16)


def join_kernel(grad_ref, *refs):
    losses, out = refs[:-1], refs[-1]
    size = grad_ref.shape[0]
    loss = losses[0][...]
    if len(losses) == 4:
        loss = (loss + losses[2][...]) + (losses[1][...] + losses[3][...])
    out[:size, :] = grad_ref[...]
    row = lax.broadcasted_iota(jnp.int32, (8, LANES), 0)
    high = loss.astype(jnp.bfloat16).astype(jnp.float32)
    middle = (loss - high).astype(jnp.bfloat16).astype(jnp.float32)
    low = (loss - high) - middle
    parts = jnp.where(row == 0, high, jnp.where(row == 1, middle, jnp.where(row == 2, low, 0.0)))
    out[size:, :] = jnp.concatenate([parts, parts], axis=0).astype(jnp.bfloat16)


def final_kernel(seq_count, per_place, *refs):
    pieces = refs[:seq_count]
    grad_ref, loss_ref, parts_s = refs[seq_count:]
    for shift, piece in enumerate(pieces):
        source = place_of(shift, seq_count)
        for chunk in range(per_place):
            grad_ref[source * per_place + chunk] = piece[
                chunk * LANES : (chunk + 1) * LANES, :
            ].astype(jnp.float32)
        tail = piece[per_place * LANES :, :].astype(jnp.float32)
        parts_s[source] = tail[0:1, :] + tail[1:2, :] + tail[2:3, :]
    loss = parts_s[0]
    for source in range(1, seq_count):
        loss = loss + parts_s[source]
    loss_ref[...] = loss


def kernel_call(
    kernel, out_shape, scratch_shapes, flops, moved, name, vmem=48, **specs
):
    return pl.pallas_call(
        kernel,
        **specs,
        out_shape=out_shape,
        scratch_shapes=scratch_shapes,
        compiler_params=pltpu.CompilerParams(vmem_limit_bytes=vmem * 1024 * 1024),
        cost_estimate=pl.CostEstimate(flops=flops, bytes_accessed=moved, transcendentals=0),
        name=name,
    )


def split_body(queries, keys, values, documents, feature_map):
    tok_rows, head_count, head_width = queries.shape
    seq_count = lax.axis_size("seq")
    per_place = head_count // seq_count
    total = tok_rows * seq_count
    score_scale = head_width ** (-0.5)
    normaliser = 1.0 / (total * head_count * lax.axis_size(("grp", "head")))
    flat = [a.reshape(tok_rows * head_count, head_width) for a in (queries, keys, values)]
    docs = documents.reshape(1, tok_rows)
    sent_rows = 3 * tok_rows + META_ROWS
    bf16, f32 = jnp.bfloat16, jnp.float32

    def sizes(*rows, dtype=bf16):
        return [jax.ShapeDtypeStruct((n, LANES), dtype) for n in rows]

    def sent(blocks):
        return [blocks[0]] + [turned(blocks[d], "seq", d) for d in range(1, seq_count)]

    def after(blocks, arrived):
        blocks, passed = lax.optimization_barrier((blocks, arrived[1:]))
        return blocks, arrived[:1] + passed

    first_parts = [(0, shift) for shift in range(1, seq_count)]
    later_parts = [(0, 0)] + [
        (chunk, shift) for chunk in range(1, per_place) for shift in range(seq_count)
    ]
    wide = pltpu.VMEM((3, tok_rows * head_count, LANES), f32)
    first_packed = kernel_call(
        functools.partial(pack_kernel, seq_count, per_place, first_parts),
        sizes(*[sent_rows] * len(first_parts)),
        [
            pltpu.VMEM((3, tok_rows * head_count, LANES), bf16),
            wide,
            pltpu.VMEM((1, tok_rows), jnp.int32),
            pltpu.SemaphoreType.DMA((3 * COPIES + 1,)),
        ],
        0,
        12 * tok_rows * head_count * LANES,
        "pack",
        vmem=PACK_VMEM,
        in_specs=[pl.BlockSpec(memory_space=pltpu.HBM)] * 4,
    )(*flat, docs)
    *packed, own_map = kernel_call(
        functools.partial(pack_rest_kernel, seq_count, per_place, later_parts),
        sizes(*[sent_rows] * len(later_parts))
        + [jax.ShapeDtypeStruct((per_place,) + feature_map.shape[1:], f32)],
        [wide],
        0,
        12 * tok_rows * head_count * LANES,
        "pack_rest",
    )(*flat, docs, feature_map)
    held = [sent(packed[:1] + list(first_packed))]
    for chunk in range(1, per_place):
        held.append(sent(packed[1 + (chunk - 1) * seq_count : 1 + chunk * seq_count]))

    returned, saved = [], []
    loss = jnp.zeros((8, LANES), f32)
    for chunk in range(per_place):
        results = kernel_call(
            functools.partial(forward_kernel, seq_count, chunk, score_scale, normaliser),
            sizes(*[2 * tok_rows] * seq_count)
            + sizes(8, dtype=f32)
            + [
                jax.ShapeDtypeStruct((3, total, LANES), bf16),
                jax.ShapeDtypeStruct((2, total, LANES), f32),
                jax.ShapeDtypeStruct((total, 2 * LANES), bf16),
                jax.ShapeDtypeStruct((META_ROWS, LANES), jnp.int32),
            ],
            [
                pltpu.VMEM((total, 2 * LANES), bf16),
                pltpu.VMEM((total, LANES), bf16),
                pltpu.VMEM((total, LANES), bf16),
                pltpu.VMEM((total, LANES), bf16),
                pltpu.VMEM((total, LANES), bf16),
            ],
            HEAD_COST,
            16 * total * LANES,
            "forward",
        )(*held[chunk], own_map, loss)
        loss = results[seq_count]
        saved.append(results[seq_count + 1 :])
        returned.append(sent(results[:seq_count]))

    saved, returned[0] = after(saved, returned[0])
    grad = kernel_call(
        functools.partial(backward_kernel, per_place),
        sizes(per_place * LANES)[0],
        [
            pltpu.VMEM((total, 2 * LANES), bf16),
            pltpu.VMEM((total, LANES), bf16),
            pltpu.VMEM((total, LANES), bf16),
            pltpu.VMEM((total, LANES), f32),
            pltpu.VMEM((total, LANES), f32),
        ],
        HEAD_COST,
        16 * total * LANES,
        "backward",
    )(*[part for parts in saved for part in parts])
    loss = summed_over(loss, "grp")
    if lax.axis_size("head") == 4:
        losses = [loss] + [crossed(loss, "head", mask) for mask in range(1, 4)]
    else:
        losses = [summed_over(loss, "head")]
    joined = kernel_call(
        join_kernel,
        sizes(per_place * LANES + META_ROWS)[0],
        [],
        0,
        16 * LANES * LANES,
        "join",
    )(grad, *losses)
    last = [joined]
    for shift in range(1, seq_count):
        behind = [pieces[shift] for pieces in returned[1:]]
        block, behind = lax.optimization_barrier((joined, behind))
        for pieces, piece in zip(returned[1:], behind):
            pieces[shift] = piece
        last.append(turned(block, "seq", shift))
    teacher_out, student_out = kernel_call(
        functools.partial(unpack_kernel, seq_count, per_place),
        sizes(*[tok_rows * head_count] * 2),
        [pltpu.VMEM((tok_rows * head_count, LANES), f32)] * 2,
        0,
        12 * tok_rows * head_count * LANES,
        "unpack",
    )(*[piece for pieces in returned for piece in pieces])
    feature_grad, loss = kernel_call(
        functools.partial(final_kernel, seq_count, per_place),
        [jax.ShapeDtypeStruct(feature_map.shape, f32)] + sizes(1, dtype=f32),
        [pltpu.VMEM((seq_count, 1, LANES), f32)],
        0,
        8 * head_count * LANES * LANES,
        "final",
    )(*last)
    return (
        teacher_out.reshape(queries.shape),
        student_out.reshape(queries.shape),
        loss[0, 0],
        feature_grad,
    )


def body(queries, keys, values, documents, feature_map):
    tok_rows, head_count, head_width = queries.shape
    if fits_split(tok_rows, head_count, head_width, feature_map.shape[2], lax.axis_size("seq")):
        return split_body(queries, keys, values, documents, feature_map)
    return relay_body(queries, keys, values, documents, feature_map)


def solution(mesh):
    in_specs = (
        P("seq", ("grp", "head"), None),
        P("seq", ("grp", "head"), None),
        P("seq", ("grp", "head"), None),
        P("seq"),
        P(("grp", "head"), None, None),
    )
    out_specs = (
        P("seq", ("grp", "head"), None),
        P("seq", ("grp", "head"), None),
        P(),
        P(("grp", "head"), None, None),
    )
    return jax.shard_map(body, mesh=mesh, in_specs=in_specs, out_specs=out_specs, check_vma=False)
```

```python
import functools
import math

import jax
import jax.numpy as jnp
from jax import lax
from jax.experimental import pallas as pl
from jax.experimental.pallas import tpu as pltpu
from jax.sharding import PartitionSpec as P

WINDOW = 64
DOC_VALUES = 4
LANES = 128
META_ROWS = 16
BLOCK = 256
LOG2E = math.log2(math.e)
COPIES = 4

PACK_VMEM = 60
HEAD_COST = 6_000_000_000


exact_mode = lax.Precision.HIGHEST
masked_value = -1e30


def passed_along(block, axis, distance):
    devices = range(lax.axis_size(axis))
    route = [(i - distance, i) for i in devices if i - distance in devices]
    return lax.ppermute(block, axis, route)


def features(inputs, weights):
    logits = jnp.einsum("rhd,hdf->rhf", inputs, weights, precision=exact_mode)
    return jnp.concatenate(
        [jax.nn.softmax(logits, axis=-1), jax.nn.softmax(-logits, axis=-1)], axis=-1
    )


def join_up(earlier, later):
    merged_tag = jnp.maximum(earlier[0], later[0])
    early_keep = (earlier[0] == merged_tag).astype(earlier[1].dtype)
    late_keep = (later[0] == merged_tag).astype(later[1].dtype)
    return (
        merged_tag,
        early_keep * earlier[1] + late_keep * later[1],
        early_keep * earlier[2] + late_keep * later[2],
    )


def join_down(earlier, later):
    merged_tag = jnp.minimum(earlier[0], later[0])
    early_keep = (earlier[0] == merged_tag).astype(earlier[1].dtype)
    late_keep = (later[0] == merged_tag).astype(later[1].dtype)
    return (
        merged_tag,
        early_keep * earlier[1] + late_keep * later[1],
        early_keep * earlier[2] + late_keep * later[2],
    )


def relay_body(queries, keys, values, documents, feature_map):
    tok_rows, head_count, head_width = queries.shape
    half_feat = feature_map.shape[2] // 2
    score_scale = head_width ** (-0.5)
    seq_place = lax.axis_index("seq")
    seq_count = lax.axis_size("seq")
    first_row = seq_place * tok_rows
    doc_float = documents.astype(jnp.float32)
    doc_marks = (documents + 1).astype(jnp.bfloat16)
    query_pos = first_row + jnp.arange(tok_rows)

    def attend(carried, portion):
        key_piece, value_piece, mark_piece = portion
        key_pos = jnp.arange(key_piece.shape[0])
        same_doc = mark_piece.astype(jnp.float32)[None, :] - 1.0 == doc_float[:, None]
        allowed = (same_doc & (key_pos[None, :] <= query_pos[:, None]))[:, None, :]
        scores = (
            jnp.einsum("ihd,jhd->ihj", queries, key_piece, preferred_element_type=jnp.float32)
            * score_scale
        )
        scores = jnp.where(allowed, scores, masked_value)
        row_max, totals, numerator = carried
        new_max = jnp.maximum(row_max, jnp.max(scores, axis=-1))
        probabilities = jnp.where(allowed, jnp.exp(scores - new_max[:, :, None]), 0.0)
        totals = jnp.sum(probabilities, axis=-1)
        numerator = jnp.einsum(
            "ihj,jhd->ihd",
            probabilities.astype(jnp.bfloat16),
            value_piece,
            preferred_element_type=jnp.float32,
        )
        return (new_max, totals, numerator)

    start_carry = (
        jnp.full((tok_rows, head_count), masked_value, jnp.float32),
        jnp.zeros((tok_rows, head_count), jnp.float32),
        jnp.zeros((tok_rows, head_count, head_width), jnp.float32),
    )
    portion = (
        lax.all_gather(keys, "seq", axis=0, tiled=True),
        lax.all_gather(values, "seq", axis=0, tiled=True),
        lax.all_gather(doc_marks, "seq", axis=0, tiled=True),
    )
    touches = (jnp.int32(0) < first_row + tok_rows) & (
        portion[2][-1].astype(jnp.float32) - 1.0 >= doc_float[0]
    )

    def compute_update(held_carry):
        return attend(held_carry, portion)

    def keep_carry(held_carry):
        return held_carry

    row_max, totals, numerator = lax.cond(touches, compute_update, keep_carry, start_carry)
    teacher_out = (numerator / totals[:, :, None]).astype(jnp.bfloat16)
    target = teacher_out.astype(jnp.float32)
    halo_keys, halo_values, halo_marks = passed_along(
        (keys[tok_rows - WINDOW :], values[tok_rows - WINDOW :], doc_marks[tok_rows - WINDOW :]),
        "seq",
        1,
    )
    key_joined = jnp.concatenate([halo_keys, keys], axis=0)
    key_float = key_joined.astype(jnp.float32)
    value_float = jnp.concatenate([halo_values, values], axis=0).astype(jnp.float32)
    doc_all = jnp.concatenate([halo_marks.astype(jnp.float32) - 1.0, doc_float], axis=0)
    query_float = queries.astype(jnp.float32)
    distance = jnp.arange(tok_rows)[:, None] + WINDOW - jnp.arange(tok_rows + WINDOW)[None, :]
    same_doc = doc_float[:, None] == doc_all[None, :]
    in_window = same_doc & (distance >= 0) & (distance < WINDOW)
    beyond = same_doc & (distance >= WINDOW)
    scores = (
        jnp.einsum("ihd,jhd->hij", queries, key_joined, preferred_element_type=jnp.float32)
        * score_scale
    )
    window_row = jnp.max(jnp.where(in_window[None], scores, masked_value), axis=-1, keepdims=True)
    window_weight = jnp.where(in_window[None], jnp.exp(scores - window_row), 0.0)
    elem_keys = key_float[:tok_rows]
    elem_values = value_float[:tok_rows]
    elem_docs = doc_all[:tok_rows]
    elem_tag = elem_docs[tok_rows - 1]
    in_tail = (elem_docs == elem_tag).astype(jnp.float32)

    def element(weights):
        masked_feat = features(elem_keys, weights[:, :, half_feat:]) * in_tail[:, None, None]
        return (
            jnp.einsum("jhf,jhd->hfd", masked_feat, elem_values, precision=exact_mode),
            jnp.sum(masked_feat, axis=0),
        )

    (elem_state, elem_norm), element_pullback = jax.vjp(element, feature_map)
    blank_state = jnp.zeros_like(elem_state)
    blank_norm = jnp.zeros_like(elem_norm)
    forward_blank = (jnp.float32(-2.0), blank_state, blank_norm)

    def relay_step(turn_index, carried):
        arrived = passed_along(join_up(carried, (elem_tag, elem_state, elem_norm)), "seq", 1)
        return jax.tree.map(
            lambda received, blank_entry: jnp.where(seq_place == 0, blank_entry, received),
            arrived,
            forward_blank,
        )

    tag_in, state_in, norm_in = lax.fori_loop(0, seq_count - 1, relay_step, forward_blank)
    uses_state = (doc_float == tag_in).astype(jnp.float32)[:, None]
    normaliser = 1.0 / (tok_rows * seq_count * head_count * lax.axis_size(("grp", "head")))

    def local_loss(weights, state, norm):
        query_feat = features(query_float, weights[:, :, :half_feat])
        key_feat = features(key_float, weights[:, :, half_feat:])
        linear = jnp.where(
            beyond[None],
            jnp.einsum("ihf,jhf->hij", query_feat, key_feat, precision=exact_mode),
            0.0,
        )
        weight = window_weight + linear
        numer_sum = jnp.einsum("hij,jhd->ihd", weight, value_float, precision=exact_mode)
        numer_sum = numer_sum + uses_state[:, :, None] * jnp.einsum(
            "ihf,hfd->ihd", query_feat, state, precision=exact_mode
        )
        denominator = jnp.sum(weight, axis=-1).T + uses_state * jnp.einsum(
            "ihf,hf->ih", query_feat, norm, precision=exact_mode
        )
        output = numer_sum / denominator[:, :, None]
        return (jnp.sum(jnp.square(output - target)) * normaliser, output)

    local_part, local_pullback, output = jax.vjp(
        local_loss, feature_map, state_in, norm_in, has_aux=True
    )
    grad_direct, grad_state, grad_norm = local_pullback(jnp.ones_like(local_part))
    backward_blank = (jnp.float32(1000000000.0), blank_state, blank_norm)

    def return_step(turn_index, carried):
        arrived = passed_along(join_down(carried, (tag_in, grad_state, grad_norm)), "seq", -1)
        return jax.tree.map(
            lambda received, blank_entry: jnp.where(
                seq_place == seq_count - 1, blank_entry, received
            ),
            arrived,
            backward_blank,
        )

    back_tag, carried_state, carried_norm = lax.fori_loop(
        0, seq_count - 1, return_step, backward_blank
    )
    total_grad = grad_direct + element_pullback((carried_state, carried_norm))[0]
    feature_grad = lax.psum(total_grad, "seq")
    loss_total = lax.psum(local_part, ("grp", "seq", "head"))
    return (teacher_out, output.astype(jnp.bfloat16), loss_total, feature_grad)


def turned(block, axis, distance):
    count = lax.axis_size(axis)
    return lax.ppermute(block, axis, [(i, (i + distance) % count) for i in range(count)])


def crossed(block, axis, mask):
    count = lax.axis_size(axis)
    return lax.ppermute(block, axis, [(i, i ^ mask) for i in range(count)])


def summed_over(block, axis):
    count = lax.axis_size(axis)
    if count == 1:
        return block
    if count == 2:
        return block + crossed(block, axis, 1)
    if count == 4:
        return (block + crossed(block, axis, 2)) + (
            crossed(block, axis, 1) + crossed(block, axis, 3)
        )
    return lax.psum(block, axis)


def fits_split(tok_rows, head_count, head_width, feat, seq_count):
    return (
        head_count % seq_count == 0
        and head_count % 8 == 0
        and tok_rows % 16 == 0
        and tok_rows <= 256
        and tok_rows * seq_count <= 1536
        and (tok_rows * seq_count) % BLOCK == 0
        and head_width == LANES
        and feat == LANES
    )


def dot_nn(a, b):
    return jnp.dot(a, b, preferred_element_type=jnp.float32)


def dot_nt(a, b):
    return lax.dot_general(a, b, (((1,), (1,)), ((), ())), preferred_element_type=jnp.float32)


def dot_tn(a, b):
    return lax.dot_general(a, b, (((0,), (0,)), ((), ())), preferred_element_type=jnp.float32)


def place_of(shift, seq_count):
    return lax.rem(lax.axis_index("seq") + (seq_count - shift), seq_count)


def deal(wide, docs, parts, outs, seq_count, per_place):
    rows = docs.shape[1]
    heads = seq_count * per_place
    meta_row = lax.broadcasted_iota(jnp.int32, (META_ROWS, LANES), 0)
    meta = jnp.zeros((META_ROWS, LANES), jnp.float32)
    for value in range(DOC_VALUES - 1):
        amount = jnp.sum((docs <= value).astype(jnp.float32), axis=1, keepdims=True)
        meta = jnp.where(meta_row == value, amount, meta)
    for (chunk, shift), out in zip(parts, outs):
        head = lax.rem(lax.axis_index("seq") + shift, seq_count) * per_place + chunk
        for n in range(3):
            out[n * rows : (n + 1) * rows, :] = wide[
                n, pl.ds(head, rows, stride=heads), :
            ].astype(jnp.bfloat16)
        out[3 * rows :, :] = meta.astype(jnp.bfloat16)


def pack_kernel(seq_count, per_place, parts, q_ref, k_ref, v_ref, doc_ref, *rest):
    outs, (narrow, wide, docs, sems) = rest[: len(parts)], rest[len(parts) :]
    part = narrow.shape[1] // COPIES
    copies = []
    for n, ref in enumerate((q_ref, k_ref, v_ref)):
        for piece in range(COPIES):
            span = pl.ds(piece * part, part)
            copies.append(
                pltpu.make_async_copy(
                    ref.at[span, :], narrow.at[n, span, :], sems.at[n * COPIES + piece]
                )
            )
    copies.append(pltpu.make_async_copy(doc_ref, docs, sems.at[3 * COPIES]))
    for copy in copies:
        copy.start()
    for n in range(3):
        for piece in range(COPIES):
            copies[n * COPIES + piece].wait()
            span = pl.ds(piece * part, part)
            wide[n, span, :] = narrow[n, span, :].astype(jnp.float32)
    copies[-1].wait()
    deal(wide, docs[...], parts, outs, seq_count, per_place)


def pack_rest_kernel(seq_count, per_place, parts, q_ref, k_ref, v_ref, doc_ref, map_ref, *rest):
    outs, (own_map, wide) = rest[: len(parts)], rest[len(parts) :]
    for n, ref in enumerate((q_ref, k_ref, v_ref)):
        wide[n, : ref.shape[0], :] = ref[...].astype(jnp.float32)
    deal(wide, doc_ref[...], parts, outs, seq_count, per_place)
    for chunk in range(per_place):
        own_map[chunk] = map_ref[lax.axis_index("seq") * per_place + chunk]


def two_parts(array, axis):
    high = array.astype(jnp.bfloat16)
    low = (array - high.astype(jnp.float32)).astype(jnp.bfloat16)
    return jnp.concatenate([high, low], axis=axis)


def half_sums(array, ones_block):
    return dot_nn(two_parts(array, 1), ones_block)


def signed_features(inputs, weights, ones_block, left):
    logits = dot_nn(jnp.concatenate([inputs, inputs], axis=1), two_parts(weights, 0))
    left_most = jnp.max(jnp.where(left, logits, -jnp.inf), axis=1, keepdims=True)
    right_most = jnp.max(jnp.where(left, -jnp.inf, logits), axis=1, keepdims=True)
    raised = jnp.exp2((logits - jnp.where(left, left_most, right_most)) * LOG2E)
    return raised / half_sums(raised, ones_block)


def ones_halves():
    row = lax.broadcasted_iota(jnp.int32, (2 * LANES, LANES), 0) % LANES < LANES // 2
    col = lax.broadcasted_iota(jnp.int32, (2 * LANES, LANES), 1) < LANES // 2
    return (row == col).astype(jnp.bfloat16)


def block_places(first, bounds):
    place = lax.broadcasted_iota(jnp.int32, (BLOCK, LANES), 0) + first
    start = jnp.zeros((BLOCK, LANES), jnp.int32)
    for value in range(DOC_VALUES - 1):
        bound = bounds[value : value + 1, :]
        start = jnp.maximum(start, jnp.where(bound <= place, bound, 0))
    return place[:, :1], start[:, :1]


def forward_kernel(seq_count, chunk, score_scale, normaliser, *refs):
    pieces, map_ref, earlier_ref = refs[:seq_count], refs[seq_count], refs[seq_count + 1]
    outs = refs[seq_count + 2 : 2 * seq_count + 2]
    loss_ref, qkv_ref, feat_ref, slope_ref, bound_ref = refs[
        2 * seq_count + 2 : 2 * seq_count + 7
    ]
    v_s, t_s, s_s, qb_s, kb_s = refs[2 * seq_count + 7 :]
    q_s, k_s = qkv_ref.at[0], qkv_ref.at[1]
    total = v_s.shape[0]
    rows = total // seq_count
    exponent = score_scale * LOG2E

    counts = jnp.zeros((META_ROWS, LANES), jnp.float32)
    for shift, piece in enumerate(pieces):
        span = pl.ds(pl.multiple_of(place_of(shift, seq_count) * rows, 16), rows)
        for n in range(3):
            qkv_ref[n, span, :] = piece[n * rows : (n + 1) * rows, :]
        v_s[span, :LANES] = piece[2 * rows : 3 * rows, :]
        counts = counts + piece[3 * rows :, :].astype(jnp.float32)
    v_s[:, LANES:] = jnp.ones((total, LANES), jnp.bfloat16)
    bounds = counts.astype(jnp.int32)
    bound_ref[...] = bounds

    lane = lax.broadcasted_iota(jnp.int32, (1, LANES), 1)
    left = lane < LANES // 2
    ones_block = ones_halves()
    weights = map_ref[chunk]
    rolled = pltpu.roll(weights, LANES // 2, 1)
    q_feat = signed_features(q_s[...], jnp.where(left, weights, -rolled), ones_block, left)
    k_feat = signed_features(k_s[...], jnp.where(left, rolled, -weights), ones_block, left)
    feat_ref[0] = q_feat
    feat_ref[1] = k_feat
    qb_s[...] = q_feat.astype(jnp.bfloat16)
    kb_s[...] = k_feat.astype(jnp.bfloat16)
    loss = jnp.zeros((8, LANES), jnp.float32)

    for first in range(0, total, BLOCK):
        last = first + BLOCK
        near = max(0, first - LANES)
        row, start = block_places(first, bounds)
        col = lax.broadcasted_iota(jnp.int32, (BLOCK, last), 1)
        visible = (col <= row) & (col >= start)
        far = (col <= row - WINDOW) & (col >= start)
        window = visible[:, near:] & (col[:, near:] > row - WINDOW)
        scores = dot_nt(q_s[first:last, :], k_s[:last, :])
        shown = jnp.where(visible, scores, masked_value)
        raised = jnp.exp2((shown - jnp.max(shown, axis=1, keepdims=True)) * exponent)
        numer = dot_nn(raised.astype(jnp.bfloat16), v_s[:last, :LANES])
        teacher = (numer / jnp.sum(raised, axis=1, keepdims=True)).astype(jnp.bfloat16)
        t_s[first:last, :] = teacher

        shown = jnp.where(window, scores[:, near:], masked_value)
        raised = jnp.exp2((shown - jnp.max(shown, axis=1, keepdims=True)) * exponent)
        linear = dot_nt(qb_s[first:last, :], kb_s[:last, :])
        weight = jnp.where(far[:, near:], linear[:, near:], raised)
        if near:
            weight = jnp.concatenate(
                [jnp.where(far[:, :near], linear[:, :near], 0.0), weight], axis=1
            )
        sums = dot_nn(weight.astype(jnp.bfloat16), v_s[:last, :])
        inverse = 1.0 / sums[:, LANES:]
        output = sums[:, :LANES] * inverse
        s_s[first:last, :] = output.astype(jnp.bfloat16)
        error = output - teacher.astype(jnp.float32)
        loss = loss + jnp.sum((error * error).reshape(BLOCK // 8, 8, LANES), axis=0)

        slope = error * (2.0 * normaliser)
        slope_denom = -jnp.sum(slope * output, axis=1, keepdims=True) * inverse
        high = slope_denom.astype(jnp.bfloat16).astype(jnp.float32)
        extra = jnp.where(lane == 0, high, jnp.where(lane == 1, slope_denom - high, 0.0))
        slope_ref[first:last, :LANES] = (slope * inverse).astype(jnp.bfloat16)
        slope_ref[first:last, LANES:] = extra.astype(jnp.bfloat16)

    for shift, out in enumerate(outs):
        first = lax.rem(lax.axis_index("seq") + shift, seq_count) * rows
        span = pl.ds(pl.multiple_of(first, 16), rows)
        out[:rows, :] = t_s[span, :]
        out[rows:, :] = s_s[span, :]
    loss_ref[...] = earlier_ref[...] + jnp.sum(loss) * normaliser


def backward_kernel(qkv_ref, feat_ref, slope_ref, bound_ref, *refs):
    *blocks, v_s, qb_s, kb_s, dq_s, dk_s = refs
    results, outs = blocks[: len(blocks) // 2], blocks[len(blocks) // 2 :]
    total = v_s.shape[0]
    left = lax.broadcasted_iota(jnp.int32, (1, LANES), 1) < LANES // 2
    ones_block = ones_halves()

    def logits_slope(feat, slope):
        product = feat * slope
        return (product - feat * half_sums(product, ones_block)).astype(jnp.bfloat16)

    bounds = bound_ref[...]
    v_s[:, :LANES] = qkv_ref[2]
    v_s[:, LANES:] = jnp.ones((total, LANES), jnp.bfloat16)
    qb_s[...] = feat_ref[0].astype(jnp.bfloat16)
    kb_s[...] = feat_ref[1].astype(jnp.bfloat16)
    dk_s[...] = jnp.zeros_like(dk_s)
    for first in range(0, total, BLOCK):
        last = first + BLOCK
        row, start = block_places(first, bounds)
        col = lax.broadcasted_iota(jnp.int32, (BLOCK, last), 1)
        far = (col <= row - WINDOW) & (col >= start)
        slope_weight = jnp.where(
            far, dot_nt(slope_ref[first:last, :], v_s[:last, :]), 0.0
        ).astype(jnp.bfloat16)
        dq_s[first:last, :] = dot_nn(slope_weight, kb_s[:last, :])
        dk_s[:last, :] += dot_tn(slope_weight, qb_s[first:last, :])
    from_q = dot_tn(qkv_ref[0], logits_slope(feat_ref[0], dq_s[...]))
    from_k = dot_tn(qkv_ref[1], logits_slope(feat_ref[1], dk_s[...]))
    grad = jnp.where(
        left,
        from_q - pltpu.roll(from_q, LANES // 2, 1),
        pltpu.roll(from_k, LANES // 2, 1) - from_k,
    ).astype(jnp.bfloat16)
    for out in outs:
        out[out.shape[0] - LANES :, :] = grad
    for result, out in zip(results, outs):
        out[: result.shape[0], :] = result[...]


def unpack_kernel(seq_count, per_place, *refs):
    pieces = refs[: seq_count * per_place]
    t_ref, s_ref, t_wide, s_wide = refs[seq_count * per_place :]
    heads = seq_count * per_place
    rows = t_ref.shape[0] // heads
    for chunk in range(per_place):
        for shift in range(seq_count):
            piece = pieces[chunk * seq_count + shift]
            head = place_of(shift, seq_count) * per_place + chunk
            t_wide[pl.ds(head, rows, stride=heads), :] = piece[:rows, :].astype(jnp.float32)
            s_wide[pl.ds(head, rows, stride=heads), :] = piece[rows : 2 * rows, :].astype(
                jnp.float32
            )
    t_ref[...] = t_wide[: rows * heads, :].astype(jnp.bfloat16)
    s_ref[...] = s_wide[: rows * heads, :].astype(jnp.bfloat16)


def join_kernel(grad_ref, *refs):
    losses, out = refs[:-1], refs[-1]
    loss = losses[0][...]
    if len(losses) == 4:
        loss = (loss + losses[2][...]) + (losses[1][...] + losses[3][...])
    out[:LANES, :] = grad_ref[...]
    row = lax.broadcasted_iota(jnp.int32, (8, LANES), 0)
    high = loss.astype(jnp.bfloat16).astype(jnp.float32)
    middle = (loss - high).astype(jnp.bfloat16).astype(jnp.float32)
    low = (loss - high) - middle
    parts = jnp.where(row == 0, high, jnp.where(row == 1, middle, jnp.where(row == 2, low, 0.0)))
    out[LANES:, :] = jnp.concatenate([parts, parts], axis=0).astype(jnp.bfloat16)


def final_kernel(seq_count, per_place, *refs):
    pieces = refs[: seq_count * per_place]
    grad_ref, loss_ref, parts_s = refs[seq_count * per_place :]
    for shift in range(seq_count):
        source = place_of(shift, seq_count)
        for chunk in range(per_place - 1):
            piece = pieces[chunk * seq_count + shift]
            grad_ref[source * per_place + chunk] = piece[
                piece.shape[0] - LANES :, :
            ].astype(jnp.float32)
        piece = pieces[(per_place - 1) * seq_count + shift]
        grad_ref[source * per_place + per_place - 1] = piece[:LANES, :].astype(jnp.float32)
        tail = piece[LANES:, :].astype(jnp.float32)
        parts_s[source] = tail[0:1, :] + tail[1:2, :] + tail[2:3, :]
    loss = parts_s[0]
    for source in range(1, seq_count):
        loss = loss + parts_s[source]
    loss_ref[...] = loss


def kernel_call(
    kernel, out_shape, scratch_shapes, flops, moved, name, vmem=48, **specs
):
    return pl.pallas_call(
        kernel,
        **specs,
        out_shape=out_shape,
        scratch_shapes=scratch_shapes,
        compiler_params=pltpu.CompilerParams(vmem_limit_bytes=vmem * 1024 * 1024),
        cost_estimate=pl.CostEstimate(flops=flops, bytes_accessed=moved, transcendentals=0),
        name=name,
    )


def split_body(queries, keys, values, documents, feature_map):
    tok_rows, head_count, head_width = queries.shape
    seq_count = lax.axis_size("seq")
    per_place = head_count // seq_count
    total = tok_rows * seq_count
    score_scale = head_width ** (-0.5)
    normaliser = 1.0 / (total * head_count * lax.axis_size(("grp", "head")))
    flat = [a.reshape(tok_rows * head_count, head_width) for a in (queries, keys, values)]
    docs = documents.reshape(1, tok_rows)
    sent_rows = 3 * tok_rows + META_ROWS
    bf16, f32 = jnp.bfloat16, jnp.float32

    def sizes(*rows, dtype=bf16):
        return [jax.ShapeDtypeStruct((n, LANES), dtype) for n in rows]

    def sent(blocks):
        return [blocks[0]] + [turned(blocks[d], "seq", d) for d in range(1, seq_count)]

    def after(blocks, arrived):
        blocks, passed = lax.optimization_barrier((blocks, arrived[1:]))
        return blocks, arrived[:1] + passed

    first_parts = [(0, shift) for shift in range(1, seq_count)]
    later_parts = [(0, 0)] + [
        (chunk, shift) for chunk in range(1, per_place) for shift in range(seq_count)
    ]
    wide = pltpu.VMEM((3, (tok_rows + 1) * head_count, LANES), f32)
    first_packed = kernel_call(
        functools.partial(pack_kernel, seq_count, per_place, first_parts),
        sizes(*[sent_rows] * len(first_parts)),
        [
            pltpu.VMEM((3, tok_rows * head_count, LANES), bf16),
            wide,
            pltpu.VMEM((1, tok_rows), jnp.int32),
            pltpu.SemaphoreType.DMA((3 * COPIES + 1,)),
        ],
        0,
        12 * tok_rows * head_count * LANES,
        "pack",
        vmem=PACK_VMEM,
        in_specs=[pl.BlockSpec(memory_space=pltpu.HBM)] * 4,
    )(*flat, docs)
    *packed, own_map = kernel_call(
        functools.partial(pack_rest_kernel, seq_count, per_place, later_parts),
        sizes(*[sent_rows] * len(later_parts))
        + [jax.ShapeDtypeStruct((per_place,) + feature_map.shape[1:], f32)],
        [wide],
        0,
        12 * tok_rows * head_count * LANES,
        "pack_rest",
    )(*flat, docs, feature_map)
    held = [sent(packed[:1] + list(first_packed))]
    for chunk in range(1, per_place):
        held.append(sent(packed[1 + (chunk - 1) * seq_count : 1 + chunk * seq_count]))

    returned = []
    loss = jnp.zeros((8, LANES), f32)
    for chunk in range(per_place):
        results = kernel_call(
            functools.partial(forward_kernel, seq_count, chunk, score_scale, normaliser),
            sizes(*[2 * tok_rows] * seq_count)
            + sizes(8, dtype=f32)
            + [
                jax.ShapeDtypeStruct((3, total, LANES), bf16),
                jax.ShapeDtypeStruct((2, total, LANES), f32),
                jax.ShapeDtypeStruct((total, 2 * LANES), bf16),
                jax.ShapeDtypeStruct((META_ROWS, LANES), jnp.int32),
            ],
            [
                pltpu.VMEM((total, 2 * LANES), bf16),
                pltpu.VMEM((total, LANES), bf16),
                pltpu.VMEM((total, LANES), bf16),
                pltpu.VMEM((total, LANES), bf16),
                pltpu.VMEM((total, LANES), bf16),
            ],
            HEAD_COST,
            16 * total * LANES,
            "forward",
        )(*held[chunk], own_map, loss)
        loss, *saved = results[seq_count:]
        blocks = results[:seq_count]
        if chunk:
            saved, returned[chunk - 1] = after(saved, returned[chunk - 1])
        if chunk + 1 < per_place:
            given, rows = blocks, [2 * tok_rows + LANES] * seq_count
        else:
            returned.append(sent(blocks))
            given, rows = [], [LANES]
        grad = kernel_call(
            backward_kernel,
            sizes(*rows),
            [
                pltpu.VMEM((total, 2 * LANES), bf16),
                pltpu.VMEM((total, LANES), bf16),
                pltpu.VMEM((total, LANES), bf16),
                pltpu.VMEM((total, LANES), f32),
                pltpu.VMEM((total, LANES), f32),
            ],
            HEAD_COST,
            16 * total * LANES,
            "backward",
        )(*saved, *given)
        if chunk + 1 < per_place:
            grad, own_map = lax.optimization_barrier((grad, own_map))
            returned.append(sent(grad))


    loss = summed_over(loss, "grp")
    if lax.axis_size("head") == 4:
        losses = [loss] + [crossed(loss, "head", mask) for mask in range(1, 4)]
    else:
        losses = [summed_over(loss, "head")]
    joined = kernel_call(
        join_kernel,
        sizes(LANES + META_ROWS)[0],
        [],
        0,
        16 * LANES * LANES,
        "join",
    )(*grad, *losses)
    last = [joined]
    for shift in range(1, seq_count):
        behind = [pieces[shift] for pieces in returned[-1:]]
        block, behind = lax.optimization_barrier((joined, behind))
        for pieces, piece in zip(returned[-1:], behind):
            pieces[shift] = piece
        last.append(turned(block, "seq", shift))
    teacher_out, student_out = kernel_call(
        functools.partial(unpack_kernel, seq_count, per_place),
        sizes(*[tok_rows * head_count] * 2),
        [pltpu.VMEM(((tok_rows + 1) * head_count, LANES), f32)] * 2,
        0,
        12 * tok_rows * head_count * LANES,
        "unpack",
    )(*[piece for pieces in returned for piece in pieces])
    feature_grad, loss = kernel_call(
        functools.partial(final_kernel, seq_count, per_place),
        [jax.ShapeDtypeStruct(feature_map.shape, f32)] + sizes(1, dtype=f32),
        [pltpu.VMEM((seq_count, 1, LANES), f32)],
        0,
        8 * head_count * LANES * LANES,
        "final",
    )(*[piece for pieces in returned[:-1] for piece in pieces], *last)
    return (
        teacher_out.reshape(queries.shape),
        student_out.reshape(queries.shape),
        loss[0, 0],
        feature_grad,
    )


def body(queries, keys, values, documents, feature_map):
    tok_rows, head_count, head_width = queries.shape
    if fits_split(tok_rows, head_count, head_width, feature_map.shape[2], lax.axis_size("seq")):
        return split_body(queries, keys, values, documents, feature_map)
    return relay_body(queries, keys, values, documents, feature_map)


def solution(mesh):
    in_specs = (
        P("seq", ("grp", "head"), None),
        P("seq", ("grp", "head"), None),
        P("seq", ("grp", "head"), None),
        P("seq"),
        P(("grp", "head"), None, None),
    )
    out_specs = (
        P("seq", ("grp", "head"), None),
        P("seq", ("grp", "head"), None),
        P(),
        P(("grp", "head"), None, None),
    )
    return jax.shard_map(body, mesh=mesh, in_specs=in_specs, out_specs=out_specs, check_vma=False)
```
